512 devices in a mesh: dp: 16 (over y_lo, z), mp: 32 (over y_hi, x, core).
Axes of the slice: x: 4, y: 8 (y_hi: 4, y_lo: 2; y = y_hi * 2 + y_lo), z: 8, core: 2. Of those that a mesh axis runs over, the one named last changes fastest.
Arguments:
- inputs: bfloat16 [5120, 3072], P('dp'), may hold values from -64 to 64
- ln_gain: float32 [3072], replicated, may hold values from 0.5 to 2
- w_qkv: bfloat16 [3072, 12288], P('dp', 'mp'), may hold values from -0.109375 to 0.109375
- q_gain: float32 [128], replicated, may hold values from 0.5 to 2
- k_gain: float32 [128], replicated, may hold values from 0.5 to 2
- cotangent: bfloat16 [5120, 4096], P('dp', 'mp'), may hold values from -6 to 6
Outputs:
- grad_input: bfloat16 [5120, 3072], P('dp')
- grad_w_qkv: float32 [3072, 12288], P('dp', 'mp')
The draws below stay inside these ranges and needn't reach their ends.
All inputs are finite; a program needn't handle non-finite values.
Results may differ from the reference program's by a relative error of at most 0.033.
Values may be sent and summed in bfloat16 or wider, within the bound.
No kernel may reach another device: no remote copies, remote signals or barrier semaphores. Data moves between devices by JAX's collectives and lax.ppermute only.
A program may use at most 64 MiB of HBM per device.

```python
import math
import jax
import jax.numpy as jnp
from jax import lax

D = 3072
HEAD = 128
SEQ = 320
HEADS = 32
IMAGES = 16
TOKENS = 5120


def draw_inputs(key, part):
    key = jax.random.fold_in(key, 11)
    noise_key, row_key, col_key = jax.random.split(key, 3)
    base = jax.random.truncated_normal(noise_key, -4.0, 4.0, (TOKENS, D), jnp.float32)
    row_low = 0.1
    row_span = math.log(10.0)
    row_scale = row_low * jnp.exp(jax.random.uniform(row_key, (TOKENS, 1), jnp.float32) * row_span)
    col_scale = jnp.exp(jax.random.uniform(col_key, (1, D), jnp.float32) * math.log(10.0))
    return (base * row_scale * col_scale).astype(jnp.bfloat16)


def steps_of(rng, extent, shards, smallest, top_value):
    gain = 1.0
    for axis_at, parts in shards:
        steps = jax.random.uniform(jax.random.fold_in(jax.random.fold_in(rng, 6), axis_at), (parts,), jnp.float32, smallest / len(shards), top_value / len(shards))
        gain = gain * jnp.repeat(jnp.exp(steps), extent[axis_at] // parts).reshape((-1,) + (1,) * (len(extent) - 1 - axis_at))
    return gain


def scatter_about(own_key, shape, scale, most, cuts=(), held_as=jnp.bfloat16):
    factor_of = steps_of(own_key, shape, cuts, -0.22, 0.18) if cuts else 1.0
    entries = jax.random.normal(own_key, shape, jnp.float32) * scale * factor_of
    return jnp.minimum(jnp.maximum(entries, -most), most).astype(held_as)


def setup_inputs(seed: int = 0) -> dict:
    seeds = jax.random.split(jax.random.key(seed), 7)
    return {
        "inputs": draw_inputs(jax.random.fold_in(seeds[6], 71), 0),
        "ln_gain": jnp.clip(jnp.exp(jax.random.uniform(seeds[1], (D,), jnp.float32, math.log(0.5), math.log(2.0))), 0.5, 2.0),
        "w_qkv": scatter_about(seeds[2], (D, HEADS * 3 * HEAD), D ** -0.5, 0.109375, ((0, 16), (1, 32))),
        "q_gain": jnp.clip(jnp.exp(jax.random.uniform(seeds[3], (HEAD,), jnp.float32, math.log(0.5), math.log(2.0))), 0.5, 2.0),
        "k_gain": jnp.clip(jnp.exp(jax.random.uniform(seeds[4], (HEAD,), jnp.float32, math.log(0.5), math.log(2.0))), 0.5, 2.0),
        "cotangent": scatter_about(seeds[5], (TOKENS, HEADS * HEAD), 1.0, 6.0, ((0, 16), (1, 32))),
    }


EPSILON = 1e-06

def normalize(values):
    centred = values - lax.optimization_barrier(jnp.mean(values, axis=-1, keepdims=True))
    inverse = lax.rsqrt(lax.optimization_barrier(jnp.mean(centred * centred, axis=-1, keepdims=True)) + EPSILON)
    return (centred * inverse, inverse)

def norm_backward(grad_unit, unit_vals, inverse):
    first_mean = lax.optimization_barrier(jnp.mean(grad_unit, axis=-1, keepdims=True))
    second_mean = lax.optimization_barrier(jnp.mean(grad_unit * unit_vals, axis=-1, keepdims=True))
    return inverse * (grad_unit - first_mean - unit_vals * second_mean)

def contract(left_op, right_op, left_dim, right_dim):
    return lax.dot_general(left_op, right_op, (((left_dim,), (right_dim,)), ((), ())), preferred_element_type=jnp.float32)

def head_grads(qkv_head, cot_head, q_gain, k_gain):
    head_width = cot_head.shape[1]
    factor = 1.0 / math.sqrt(head_width)
    q_unit, q_inverse = normalize(qkv_head[:, :head_width].astype(jnp.float32))
    k_unit, k_inverse = normalize(qkv_head[:, head_width:2 * head_width].astype(jnp.float32))
    values = qkv_head[:, 2 * head_width:]
    q_normed = (q_unit * q_gain).astype(jnp.bfloat16)
    k_normed = (k_unit * k_gain).astype(jnp.bfloat16)
    scores = contract(q_normed, k_normed, 1, 1) * factor
    exp_scores = jnp.exp(scores)
    attn_weights = exp_scores / lax.optimization_barrier(jnp.sum(exp_scores, axis=-1, keepdims=True))
    grad_attn = contract(cot_head, values, 1, 1)
    centre = lax.optimization_barrier(jnp.sum(attn_weights * grad_attn, axis=-1, keepdims=True))
    grad_scores = (attn_weights * (grad_attn - centre)).astype(jnp.bfloat16)
    grad_values = contract(attn_weights.astype(jnp.bfloat16), cot_head, 0, 0)
    grad_query = norm_backward(contract(grad_scores, k_normed, 1, 0) * factor * q_gain, q_unit, q_inverse)
    grad_key = norm_backward(contract(grad_scores, q_normed, 0, 0) * factor * k_gain, k_unit, k_inverse)
    return jnp.concatenate([grad_query, grad_key, grad_values], axis=1).astype(jnp.bfloat16)

def reference(inputs, ln_gain, w_qkv, q_gain, k_gain, cotangent):
    x_unit, x_inverse = normalize(inputs.astype(jnp.float32))
    normed = (x_unit * ln_gain).astype(jnp.bfloat16)
    qkv_all = jnp.dot(normed, w_qkv, preferred_element_type=jnp.float32).astype(jnp.bfloat16)
    triple = 3 * HEAD
    qkv_heads = jnp.transpose(qkv_all.reshape(IMAGES, SEQ, HEADS, triple), (0, 2, 1, 3))
    cot_heads = jnp.transpose(cotangent.reshape(IMAGES, SEQ, HEADS, HEAD), (0, 2, 1, 3))

    def per_head(head_pair):
        return head_grads(head_pair[0], head_pair[1], q_gain, k_gain)

    def per_image(image_pair):
        return lax.map(per_head, image_pair)
    grad_qkv = lax.map(per_image, (qkv_heads, cot_heads))
    w_heads = jnp.transpose(w_qkv.reshape(D, HEADS, triple), (1, 0, 2))
    grad_heads = jnp.transpose(grad_qkv, (1, 0, 2, 3)).reshape(HEADS, TOKENS, triple)

    def add_head(total, head_pair):
        term = contract(head_pair[0], head_pair[1], 1, 1).astype(jnp.bfloat16)
        return (total + lax.optimization_barrier(term).astype(jnp.float32), None)
    grad_normed, unused = lax.scan(add_head, jnp.zeros((TOKENS, D), jnp.float32), (grad_heads, w_heads))
    grad_input = norm_backward(grad_normed * ln_gain, x_unit, x_inverse).astype(jnp.bfloat16)
    grad_rows = jnp.transpose(grad_qkv, (0, 2, 1, 3)).reshape(IMAGES, SEQ, HEADS * triple)
    normed_images = normed.reshape(IMAGES, SEQ, D)

    def add_image(total, image_pair):
        term = contract(image_pair[0], image_pair[1], 0, 0).astype(jnp.bfloat16)
        return (total + lax.optimization_barrier(term).astype(jnp.float32), None)
    grad_w_qkv, unused = lax.scan(add_image, jnp.zeros((D, HEADS * triple), jnp.float32), (normed_images, grad_rows))
    return (grad_input, grad_w_qkv)
```

```python
import math

import jax
import jax.numpy as jnp
from jax import lax
from jax.sharding import PartitionSpec as P

EPSILON = 1e-06


def normalize(values):
    centred = values - jnp.mean(values, axis=-1, keepdims=True)
    inverse = lax.rsqrt(jnp.mean(centred * centred, axis=-1, keepdims=True) + EPSILON)
    return (centred * inverse, inverse)


def norm_backward(grad_unit, unit_vals, inverse):
    first_mean = jnp.mean(grad_unit, axis=-1, keepdims=True)
    second_mean = jnp.mean(grad_unit * unit_vals, axis=-1, keepdims=True)
    return inverse * (grad_unit - first_mean - unit_vals * second_mean)


def contract(left_op, right_op, left_dim, right_dim):
    return lax.dot_general(
        left_op,
        right_op,
        (((left_dim,), (right_dim,)), ((), ())),
        preferred_element_type=jnp.float32,
    )


def head_grads(qkv_head, cot_head, q_gain, k_gain):
    head_width = cot_head.shape[1]
    factor = 1.0 / math.sqrt(head_width)
    q_unit, q_inverse = normalize(qkv_head[:, :head_width].astype(jnp.float32))
    k_unit, k_inverse = normalize(qkv_head[:, head_width : 2 * head_width].astype(jnp.float32))
    values = qkv_head[:, 2 * head_width :]
    q_normed = (q_unit * q_gain).astype(jnp.bfloat16)
    k_normed = (k_unit * k_gain).astype(jnp.bfloat16)
    scores = contract(q_normed, k_normed, 1, 1) * factor
    exp_scores = jnp.exp(scores)
    attn_weights = exp_scores / jnp.sum(exp_scores, axis=-1, keepdims=True)
    grad_attn = contract(cot_head, values, 1, 1)
    centre = jnp.sum(attn_weights * grad_attn, axis=-1, keepdims=True)
    grad_scores = (attn_weights * (grad_attn - centre)).astype(jnp.bfloat16)
    grad_values = contract(attn_weights.astype(jnp.bfloat16), cot_head, 0, 0)
    grad_query = norm_backward(
        contract(grad_scores, k_normed, 1, 0) * factor * q_gain, q_unit, q_inverse
    )
    grad_key = norm_backward(
        contract(grad_scores, q_normed, 0, 0) * factor * k_gain, k_unit, k_inverse
    )
    return jnp.concatenate([grad_query, grad_key, grad_values], axis=1).astype(jnp.bfloat16)


Y_LO, Z = 2, 8
Y_HI, X, CORE = 4, 4, 2


def partner_rows():
    return [(y * Z + z, (1 - y) * Z + z) for y in range(Y_LO) for z in range(Z)]


def z_groups():
    return [[y * Z + z for z in range(Z)] for y in range(Y_LO)]


def shifted(step_y, step_x, step_core):
    pairs = []
    for y in range(Y_HI):
        for x in range(X):
            for core in range(CORE):
                source = (y * X + x) * CORE + core
                target = ((y + step_y) % Y_HI * X + (x + step_x) % X) * CORE + (core + step_core) % CORE
                pairs.append((source, target))
    return pairs


def take(values, at, rows):
    return lax.dynamic_slice_in_dim(values, at * rows, rows, 0)


def scatter_sum(values, at, parts, perm_of):
    rows = values.shape[0] // parts
    sent = [
        lax.ppermute(take(values, (at + step) % parts, rows), "mp", perm_of(step))
        for step in range(1, parts)
    ]
    total = take(values, at, rows).astype(jnp.float32)
    for term in sent:
        total = total + term.astype(jnp.float32)
    return total


def gather_rows(values, at, parts, perm_of):
    rows = values.shape[0]
    whole = jnp.zeros((parts * rows, values.shape[1]), values.dtype)
    whole = lax.dynamic_update_slice_in_dim(whole, values, at * rows, 0)
    for step in range(1, parts):
        got = lax.ppermute(values, "mp", perm_of(step))
        whole = lax.dynamic_update_slice_in_dim(whole, got, (at - step) % parts * rows, 0)
    return whole


def per_device(inputs, ln_gain, w_qkv, q_gain, k_gain, cotangent):
    dp_at = lax.axis_index("dp")
    mp_at = lax.axis_index("mp")
    y_lo = dp_at // Z
    core, x_at, y_hi = mp_at % CORE, mp_at // CORE % X, mp_at // (CORE * X)
    x_unit, x_inverse = normalize(inputs.astype(jnp.float32))
    normed = (x_unit * ln_gain).astype(jnp.bfloat16)
    other = lax.ppermute(w_qkv, "dp", partner_rows())
    pair = jnp.where(y_lo == 0, jnp.stack([w_qkv, other]), jnp.stack([other, w_qkv]))
    weights = lax.all_gather(pair, "dp", axis_index_groups=z_groups())
    weights = jnp.transpose(weights, (1, 0, 2, 3)).reshape(inputs.shape[1], w_qkv.shape[1])
    qkv_local = jnp.dot(normed, weights, preferred_element_type=jnp.float32).astype(jnp.bfloat16)
    grad_qkv = head_grads(qkv_local, cotangent, q_gain, k_gain)
    grad_w_qkv = lax.psum_scatter(
        contract(normed, grad_qkv, 0, 0).astype(jnp.bfloat16), "dp", scatter_dimension=0, tiled=True
    ).astype(jnp.float32)
    by_core = lambda step: shifted(0, 0, step)
    by_x = lambda step: shifted(0, step, 0)
    by_y = lambda step: shifted(step, 0, 0)
    head_term = contract(grad_qkv, weights, 1, 1).astype(jnp.bfloat16)
    part = scatter_sum(head_term, core, CORE, by_core).astype(jnp.bfloat16)
    part = scatter_sum(part, x_at, X, by_x).astype(jnp.bfloat16)
    grad_normed = scatter_sum(part, y_hi, Y_HI, by_y)
    rows = grad_normed.shape[0]
    first = ((core * X + x_at) * Y_HI + y_hi) * rows
    own_unit, own_inverse = normalize(
        lax.dynamic_slice_in_dim(inputs, first, rows, 0).astype(jnp.float32)
    )
    own = norm_backward(grad_normed * ln_gain, own_unit, own_inverse).astype(jnp.bfloat16)
    own = gather_rows(own, y_hi, Y_HI, by_y)
    own = gather_rows(own, x_at, X, by_x)
    grad_input = gather_rows(own, core, CORE, by_core)
    return (grad_input, grad_w_qkv)


def solution(mesh):
    placed = (P("dp", None), P(), P("dp", "mp"), P(), P(), P("dp", "mp"))
    return jax.shard_map(
        per_device,
        mesh=mesh,
        in_specs=placed,
        out_specs=(P("dp", None), P("dp", "mp")),
        check_vma=False,
    )
```

```python
import math

import jax
import jax.numpy as jnp
from jax import lax
from jax.experimental import pallas as pl
from jax.experimental.pallas import tpu as pltpu
from jax.sharding import PartitionSpec as P

EPSILON = 1e-06
Y_LO, Z = 2, 8
Y_HI, X, CORE = 4, 4, 2
MP = Y_HI * X * CORE
AXES = ("dp", "mp")
Z_STEPS = (0, 1, -1, -2, 2, 3, -3, -4)


def normalize(values):
    centred = values - jnp.mean(values, axis=-1, keepdims=True)
    inverse = lax.rsqrt(jnp.mean(centred * centred, axis=-1, keepdims=True) + EPSILON)
    return (centred * inverse, inverse)


def norm_backward(grad_unit, unit_vals, inverse):
    first_mean = jnp.mean(grad_unit, axis=-1, keepdims=True)
    second_mean = jnp.mean(grad_unit * unit_vals, axis=-1, keepdims=True)
    return inverse * (grad_unit - first_mean - unit_vals * second_mean)


def contract(left_op, right_op, left_dim, right_dim):
    return lax.dot_general(
        left_op,
        right_op,
        (((left_dim,), (right_dim,)), ((), ())),
        preferred_element_type=jnp.float32,
    )


def head_grads(qkv_head, cot_head, q_gain, k_gain):
    width = cot_head.shape[1]
    factor = 1.0 / math.sqrt(width)
    q_unit, q_inverse = normalize(qkv_head[:, :width].astype(jnp.float32))
    k_unit, k_inverse = normalize(qkv_head[:, width : 2 * width].astype(jnp.float32))
    values = qkv_head[:, 2 * width :]
    q_normed = (q_unit * q_gain).astype(jnp.bfloat16)
    k_normed = (k_unit * k_gain).astype(jnp.bfloat16)

    def weights_and_grads(rows, columns, row_cot, column_cot, key_axis):
        exp_scores = jnp.exp(contract(rows, columns, 1, 1) * factor)
        attn = exp_scores / jnp.sum(exp_scores, axis=key_axis, keepdims=True)
        grad_attn = contract(row_cot, column_cot, 1, 1)
        centre = jnp.sum(attn * grad_attn, axis=key_axis, keepdims=True)
        return attn, (attn * (grad_attn - centre)).astype(jnp.bfloat16)

    _, grad_scores = weights_and_grads(q_normed, k_normed, cot_head, values, 1)
    attn_t, grad_scores_t = weights_and_grads(k_normed, q_normed, values, cot_head, 0)
    grad_values = contract(attn_t.astype(jnp.bfloat16), cot_head, 1, 0)
    grad_query = norm_backward(
        contract(grad_scores, k_normed, 1, 0) * factor * q_gain, q_unit, q_inverse
    )
    grad_key = norm_backward(
        contract(grad_scores_t, q_normed, 1, 0) * factor * k_gain, k_unit, k_inverse
    )
    return jnp.concatenate([grad_query, grad_key, grad_values], axis=1)


def swap_blocks(rows, outer, inner):
    half = rows.shape[0] // 2
    quarter = half // 2
    rows = jnp.where(outer == 1, jnp.concatenate([rows[half:], rows[:half]]), rows)
    swapped = jnp.concatenate(
        [rows[quarter:half], rows[:quarter], rows[half + quarter :], rows[half : half + quarter]]
    )
    return jnp.where(inner == 1, swapped, rows)


def head_kernel(places, normed, cot, q_gain, k_gain, *refs):
    blocks, refs = refs[:10], refs[10:]
    grad_ref, kept_ref, sent_ref, weights_out, weights, sems, out_sem = refs
    depth = blocks[0].shape[0]
    copies = []
    for ref in blocks:
        for part in range(ref.shape[0] // depth):
            at = len(copies)
            first = pl.multiple_of(places[at] * depth, depth)
            copies.append(
                pltpu.make_async_copy(
                    ref.at[pl.ds(part * depth, depth), :],
                    weights.at[pl.ds(first, depth), :],
                    sems.at[at],
                )
            )
    for copy in copies:
        copy.start()
    for copy in copies:
        copy.wait()
    out_copy = pltpu.make_async_copy(weights, weights_out, out_sem)
    out_copy.start()
    width = weights.shape[1]
    total = None
    for first in range(0, weights.shape[0], width):
        at = pl.ds(first, width)
        product = jnp.dot(normed[:, at], weights[at, :], preferred_element_type=jnp.float32)
        total = product if total is None else total + product
    grads = head_grads(total.astype(jnp.bfloat16), cot[...], q_gain[...], k_gain[...])
    grad_ref[...] = grads.astype(jnp.bfloat16)
    core, outer, inner = places[16], places[17], places[18]
    half = grads.shape[0] // 2
    low, high = grads[:half], grads[half:]
    kept = swap_blocks(jnp.where(core == 0, low, high), outer, inner)
    sent = swap_blocks(jnp.where(core == 0, high, low), inner, outer).astype(jnp.bfloat16)
    kept_ref[...] = kept.astype(jnp.bfloat16)

    for first in range(0, weights.shape[0], width):
        at = pl.ds(first, width)
        sent_ref[:, at] = contract(sent, weights[at, :], 1, 1).astype(jnp.bfloat16)
    out_copy.wait()


def run_head(places, normed, cot, q_gain, k_gain, blocks):
    tokens, features = normed.shape
    width = blocks[0].shape[1]
    in_vmem = pl.BlockSpec(memory_space=pltpu.VMEM)
    anywhere = pl.BlockSpec(memory_space=pl.ANY)
    like = lambda *shape: jax.ShapeDtypeStruct(shape, jnp.bfloat16)
    return pl.pallas_call(
        head_kernel,
        out_shape=(
            like(tokens, width),
            like(tokens // 2, width),
            like(tokens // 2, features),
            like(features, width),
        ),
        in_specs=[pl.BlockSpec(memory_space=pltpu.SMEM)] + [in_vmem] * 4 + [anywhere] * len(blocks),
        out_specs=(in_vmem, in_vmem, in_vmem, anywhere),
        scratch_shapes=[
            pltpu.VMEM((features, width), jnp.bfloat16),
            pltpu.SemaphoreType.DMA((16,)),
            pltpu.SemaphoreType.DMA,
        ],
        compiler_params=pltpu.CompilerParams(vmem_limit_bytes=40 * 2**20),
        cost_estimate=pl.CostEstimate(
            flops=3 * tokens * features * width, bytes_accessed=8 * 2**20, transcendentals=200000
        ),
        name="head",
    )(places, normed, cot, q_gain, k_gain, *blocks)


def norm_kernel(inputs, gain, out):
    unit, _ = normalize(inputs[...].astype(jnp.float32))
    out[...] = (unit * gain[...]).astype(out.dtype)


def run_norm(inputs, gain):
    in_vmem = pl.BlockSpec(memory_space=pltpu.VMEM)
    return pl.pallas_call(
        norm_kernel,
        out_shape=jax.ShapeDtypeStruct(inputs.shape, jnp.bfloat16),
        in_specs=[in_vmem, in_vmem],
        out_specs=in_vmem,
        compiler_params=pltpu.CompilerParams(vmem_limit_bytes=24 * 2**20),
        cost_estimate=pl.CostEstimate(
            flops=8 * inputs.size, bytes_accessed=4 * inputs.size, transcendentals=0
        ),
        name="norm",
    )(inputs, gain)


def terms_kernel(places, normed, grads, out, terms, sems):
    features, width = terms.shape
    depth = features // (Y_LO * Z)
    copies = []
    for first in range(0, features, width):
        at = pl.ds(first, width)
        terms[at, :] = contract(normed[:, at], grads[...], 0, 0).astype(terms.dtype)
        for block in range(first // depth, (first + width) // depth):
            to = pl.multiple_of(places[block] * depth, depth)
            copies.append(
                pltpu.make_async_copy(
                    terms.at[pl.ds(block * depth, depth), :],
                    out.at[pl.ds(to, depth), :],
                    sems.at[block],
                )
            )
            copies[-1].start()
    for copy in copies:
        copy.wait()


def run_terms(places, normed, grads):
    tokens, features = normed.shape
    width = grads.shape[1]
    in_vmem = pl.BlockSpec(memory_space=pltpu.VMEM)
    return pl.pallas_call(
        terms_kernel,
        out_shape=jax.ShapeDtypeStruct((features, width), jnp.bfloat16),
        in_specs=[pl.BlockSpec(memory_space=pltpu.SMEM), in_vmem, in_vmem],
        out_specs=pl.BlockSpec(memory_space=pl.ANY),
        scratch_shapes=[
            pltpu.VMEM((features, width), jnp.bfloat16),
            pltpu.SemaphoreType.DMA((Y_LO * Z,)),
        ],
        compiler_params=pltpu.CompilerParams(vmem_limit_bytes=32 * 2**20),
        cost_estimate=pl.CostEstimate(
            flops=2 * tokens * features * width, bytes_accessed=5 * 2**20, transcendentals=0
        ),
        name="terms",
    )(places, normed, grads)


def pairs_of(partner):
    found = []
    for y_lo in range(Y_LO):
        for z in range(Z):
            for y_hi in range(Y_HI):
                for x in range(X):
                    for core in range(CORE):
                        ends = ((y_lo, z, y_hi, x, core), partner(y_lo, z, y_hi, x, core))
                        found.append(
                            tuple(
                                ((a % Y_LO) * Z + b % Z) * MP
                                + ((c % Y_HI) * X + d % X) * CORE
                                + e % CORE
                                for a, b, c, d, e in ends
                            )
                        )
    return found


def way(at, core):
    return 1 if (at + core) % 2 == 0 else -1


def swap(values, partner):
    return lax.ppermute(values, AXES, pairs_of(partner))


def by_y_lo(a, b, c, d, e):
    return (1 - a, b, c, d, e)


def by_core(a, b, c, d, e):
    return (a, b, c, d, 1 - e)


def by_z(turn):
    return lambda a, b, c, d, e: (a, b + turn * way(b, e), c, d, e)


def by_x(turn):
    return lambda a, b, c, d, e: (a, b, c, d + turn * way(d, e), e)


def by_y_hi(turn):
    return lambda a, b, c, d, e: (a, b, c + turn * way(c, e), d, e)


def along_z(block):
    first = swap(block, by_z(1))
    second = swap(jnp.concatenate([block, first]), by_z(-1))
    third = swap(second, by_z(1))
    fourth = swap(third, by_z(-1))
    return [block, first, second, third, fourth]


def add(left, right):
    return (left.astype(jnp.float32) + right.astype(jnp.float32)).astype(jnp.bfloat16)


def after(values, earlier):
    return lax.optimization_barrier((values, earlier))[0]


def join(own, got, place):
    return jnp.concatenate([jnp.where(place == 0, own, got), jnp.where(place == 0, got, own)])


def per_device(inputs, ln_gain, w_qkv, q_gain, k_gain, cotangent):
    dp_at, mp_at = lax.axis_index("dp"), lax.axis_index("mp")
    y_lo, z = dp_at // Z, dp_at % Z
    core, x = mp_at % CORE, mp_at // CORE % X
    near, far = (x + 1) // 2 % 2, x // 2
    outer, inner = jnp.where(core == 0, near, far), jnp.where(core == 0, far, near)
    z_way = jnp.where((z + core) % 2 == 0, 1, -1)
    z_places = [(z + z_way * step) % Z for step in Z_STEPS]
    places = jnp.stack(
        [y_lo * Z + at for at in z_places]
        + [(1 - y_lo) * Z + at for at in z_places]
        + [core, outer, inner]
    ).astype(jnp.int32)

    other = swap(w_qkv, by_y_lo)
    blocks = along_z(w_qkv) + along_z(other)
    normed = run_norm(inputs, ln_gain.reshape(1, -1))
    grad_qkv, kept, sent, weights = run_head(
        places, normed, cotangent, q_gain.reshape(1, -1), k_gain.reshape(1, -1), blocks
    )

    got = swap(sent, by_core)
    part = contract(kept, weights, 1, 1)
    rows = part.shape[0] // 2
    part, other = add(part[:rows], got[:rows]), add(part[rows:], got[rows:])
    steps = (jnp.arange(Z) - z) * z_way % Z
    order = jnp.array([Z_STEPS.index(step if step in Z_STEPS else step - Z) for step in range(Z)])
    z_order = order[steps]
    term_places = jnp.stack([z_order * Y_LO, z_order * Y_LO + 1]).reshape(-1).astype(jnp.int32)
    terms = run_terms(term_places, normed, after(grad_qkv, other))
    depth = terms.shape[0] // Z
    zero, one, two, three, four = jnp.split(terms, [depth, 2 * depth, 4 * depth, 6 * depth])
    part = add(part, swap(other, by_x(1)))
    got = swap(four, by_z(-1))
    rows = rows // 2
    part, other = part[:rows], after(part[rows:], four)
    part = add(part, swap(other, by_x(-1)))

    three = add(three, after(got, part))
    got = swap(three, by_z(1))
    part = add(part, swap(part, by_y_hi(1)))
    part = after(part, three)
    grad_normed = part.astype(jnp.float32) + swap(part, by_y_hi(-1)).astype(jnp.float32)
    first = ((core * 2 + outer) * 2 + inner) * rows
    own_unit, own_inverse = normalize(
        lax.dynamic_slice_in_dim(inputs, first, rows, 0).astype(jnp.float32)
    )
    own = norm_backward(grad_normed * ln_gain, own_unit, own_inverse).astype(jnp.bfloat16)

    two = add(two, after(got, own))
    got = swap(two, by_z(-1))
    own = after(join(own, swap(own, by_x(-1)), inner), two)

    got = after(got, own)
    zero, one = add(zero, got[:depth]), add(one, got[depth:])
    got = swap(one, by_z(1))
    own = after(join(own, swap(own, by_x(1)), outer), one)

    zero = add(zero, after(got, own))
    depth = zero.shape[0] // 2
    low, high = zero[:depth], zero[depth:]
    share = swap(jnp.where(y_lo == 0, high, low), by_y_lo)
    got = swap(own, by_core)
    grad_input = lax.dynamic_update_slice_in_dim(
        jnp.concatenate([own, own]), got, (1 - core) * own.shape[0], 0
    )
    grad_w_qkv = jnp.where(y_lo == 0, low, high).astype(jnp.float32) + share.astype(jnp.float32)
    return (grad_input, grad_w_qkv)


def solution(mesh):
    placed = (P("dp", None), P(), P("dp", "mp"), P(), P(), P("dp", "mp"))
    return jax.shard_map(
        per_device,
        mesh=mesh,
        in_specs=placed,
        out_specs=(P("dp", None), P("dp", "mp")),
        check_vma=False,
    )
```

```python
import math

import jax
import jax.numpy as jnp
from jax import lax
from jax.experimental import pallas as pl
from jax.experimental.pallas import tpu as pltpu
from jax.sharding import PartitionSpec as P

EPSILON = 1e-06
Y_LO, Z = 2, 8
Y_HI, X, CORE = 4, 4, 2
MP = Y_HI * X * CORE
AXES = ("dp", "mp")
Z_STEPS = (0, 1, -1, -2, 2, 3, -3, -4)


def normalize(values):
    centred = values - jnp.mean(values, axis=-1, keepdims=True)
    inverse = lax.rsqrt(jnp.mean(centred * centred, axis=-1, keepdims=True) + EPSILON)
    return (centred * inverse, inverse)


def norm_backward(grad_unit, unit_vals, inverse):
    first_mean = jnp.mean(grad_unit, axis=-1, keepdims=True)
    second_mean = jnp.mean(grad_unit * unit_vals, axis=-1, keepdims=True)
    return inverse * (grad_unit - first_mean - unit_vals * second_mean)


def contract(left_op, right_op, left_dim, right_dim):
    return lax.dot_general(
        left_op,
        right_op,
        (((left_dim,), (right_dim,)), ((), ())),
        preferred_element_type=jnp.float32,
    )


def head_grads(qkv_head, cot_head, q_gain, k_gain):
    width = cot_head.shape[1]
    factor = 1.0 / math.sqrt(width)
    q_unit, q_inverse = normalize(qkv_head[:, :width].astype(jnp.float32))
    k_unit, k_inverse = normalize(qkv_head[:, width : 2 * width].astype(jnp.float32))
    values = qkv_head[:, 2 * width :]
    q_normed = (q_unit * q_gain).astype(jnp.bfloat16)
    k_normed = (k_unit * k_gain).astype(jnp.bfloat16)

    def weights_and_grads(rows, columns, row_cot, column_cot, key_axis):
        exp_scores = jnp.exp(contract(rows, columns, 1, 1) * factor)
        attn = exp_scores / jnp.sum(exp_scores, axis=key_axis, keepdims=True)
        grad_attn = contract(row_cot, column_cot, 1, 1)
        centre = jnp.sum(attn * grad_attn, axis=key_axis, keepdims=True)
        return attn, (attn * (grad_attn - centre)).astype(jnp.bfloat16)

    _, grad_scores = weights_and_grads(q_normed, k_normed, cot_head, values, 1)
    attn_t, grad_scores_t = weights_and_grads(k_normed, q_normed, values, cot_head, 0)
    grad_values = contract(attn_t.astype(jnp.bfloat16), cot_head, 1, 0)
    grad_query = norm_backward(
        contract(grad_scores, k_normed, 1, 0) * factor * q_gain, q_unit, q_inverse
    )
    grad_key = norm_backward(
        contract(grad_scores_t, q_normed, 1, 0) * factor * k_gain, k_unit, k_inverse
    )
    return jnp.concatenate([grad_query, grad_key, grad_values], axis=1)


def swap_blocks(rows, outer, inner):
    half = rows.shape[0] // 2
    quarter = half // 2
    rows = jnp.where(outer == 1, jnp.concatenate([rows[half:], rows[:half]]), rows)
    swapped = jnp.concatenate(
        [rows[quarter:half], rows[:quarter], rows[half + quarter :], rows[half : half + quarter]]
    )
    return jnp.where(inner == 1, swapped, rows)


def head_kernel(places, normed, cot, q_gain, k_gain, *refs):
    blocks, refs = refs[:10], refs[10:]
    grad_ref, kept_ref, next_ref, sent_ref, weights, sems = refs
    depth = blocks[0].shape[0]
    copies = []
    for ref in blocks:
        for part in range(ref.shape[0] // depth):
            at = len(copies)
            first = pl.multiple_of(places[at] * depth, depth)
            copies.append(
                pltpu.make_async_copy(
                    ref.at[pl.ds(part * depth, depth), :],
                    weights.at[pl.ds(first, depth), :],
                    sems.at[at],
                )
            )
    for copy in copies:
        copy.start()
    for copy in copies:
        copy.wait()
    width = weights.shape[1]
    total = None
    for first in range(0, weights.shape[0], width):
        at = pl.ds(first, width)
        product = jnp.dot(normed[:, at], weights[at, :], preferred_element_type=jnp.float32)
        total = product if total is None else total + product
    grads = head_grads(total.astype(jnp.bfloat16), cot[...], q_gain[...], k_gain[...])
    grad_ref[...] = grads.astype(jnp.bfloat16)
    core, outer, inner = places[16], places[17], places[18]
    half = grads.shape[0] // 2
    low, high = grads[:half], grads[half:]
    kept = swap_blocks(jnp.where(core == 0, low, high), outer, inner).astype(jnp.bfloat16)
    sent = swap_blocks(jnp.where(core == 0, high, low), inner, outer).astype(jnp.bfloat16)
    for first in range(0, weights.shape[0], width):
        at = pl.ds(first, width)
        sent_ref[:, at] = contract(sent, weights[at, :], 1, 1).astype(jnp.bfloat16)
        term = contract(kept, weights[at, :], 1, 1).astype(jnp.bfloat16)
        kept_ref[:, at] = term[: half // 2]
        next_ref[:, at] = term[half // 2 :]


def run_head(places, normed, cot, q_gain, k_gain, blocks):
    tokens, features = normed.shape
    width = blocks[0].shape[1]
    in_vmem = pl.BlockSpec(memory_space=pltpu.VMEM)
    in_hbm = pl.BlockSpec(memory_space=pltpu.HBM)
    like = lambda *shape: jax.ShapeDtypeStruct(shape, jnp.bfloat16)
    return pl.pallas_call(
        head_kernel,
        out_shape=(
            like(tokens, width),
            like(tokens // 4, features),
            like(tokens // 4, features),
            like(tokens // 2, features),
        ),
        in_specs=[pl.BlockSpec(memory_space=pltpu.SMEM)] + [in_vmem] * 4 + [in_hbm] * len(blocks),
        out_specs=(in_vmem,) * 4,
        scratch_shapes=[
            pltpu.VMEM((features, width), jnp.bfloat16),
            pltpu.SemaphoreType.DMA((16,)),
        ],
        compiler_params=pltpu.CompilerParams(vmem_limit_bytes=16 * 2**20),
        cost_estimate=pl.CostEstimate(
            flops=3 * tokens * features * width, bytes_accessed=8 * 2**20, transcendentals=200000
        ),
        name="head",
    )(places, normed, cot, q_gain, k_gain, *blocks)


def norm_kernel(inputs, gain, out):
    unit, _ = normalize(inputs[...].astype(jnp.float32))
    out[...] = (unit * gain[...]).astype(out.dtype)


def run_norm(inputs, gain):
    in_vmem = pl.BlockSpec(memory_space=pltpu.VMEM)
    return pl.pallas_call(
        norm_kernel,
        out_shape=jax.ShapeDtypeStruct(inputs.shape, jnp.bfloat16),
        in_specs=[in_vmem, in_vmem],
        out_specs=in_vmem,
        compiler_params=pltpu.CompilerParams(vmem_limit_bytes=12 * 2**20),
        cost_estimate=pl.CostEstimate(
            flops=8 * inputs.size, bytes_accessed=4 * inputs.size, transcendentals=0
        ),
        name="norm",
    )(inputs, gain)


def terms_kernel(places, normed, grads, out):
    features, width = out.shape
    depth = features // (Y_LO * Z)
    for first in range(0, features, width):
        term = contract(normed[:, pl.ds(first, width)], grads[...], 0, 0).astype(out.dtype)
        for part in range(width // depth):
            to = pl.multiple_of(places[first // depth + part] * depth, depth)
            out[pl.ds(to, depth), :] = term[part * depth : (part + 1) * depth]


def run_terms(places, normed, grads):
    tokens, features = normed.shape
    width = grads.shape[1]
    in_vmem = pl.BlockSpec(memory_space=pltpu.VMEM)
    return pl.pallas_call(
        terms_kernel,
        out_shape=jax.ShapeDtypeStruct((features, width), jnp.bfloat16),
        in_specs=[pl.BlockSpec(memory_space=pltpu.SMEM), in_vmem, in_vmem],
        out_specs=in_vmem,
        compiler_params=pltpu.CompilerParams(vmem_limit_bytes=12 * 2**20),
        cost_estimate=pl.CostEstimate(
            flops=2 * tokens * features * width, bytes_accessed=5 * 2**20, transcendentals=0
        ),
        name="terms",
    )(places, normed, grads)


def back_kernel(left, right, inputs, gain, out):
    unit, inverse = normalize(inputs[...].astype(jnp.float32))
    grads = (left[...].astype(jnp.float32) + right[...].astype(jnp.float32)) * gain[...]
    out[...] = norm_backward(grads, unit, inverse).astype(out.dtype)


def run_back(left, right, inputs, gain):
    in_vmem = pl.BlockSpec(memory_space=pltpu.VMEM)
    return pl.pallas_call(
        back_kernel,
        out_shape=jax.ShapeDtypeStruct(inputs.shape, jnp.bfloat16),
        in_specs=[in_vmem] * 4,
        out_specs=in_vmem,
        compiler_params=pltpu.CompilerParams(vmem_limit_bytes=8 * 2**20),
        cost_estimate=pl.CostEstimate(
            flops=20 * inputs.size, bytes_accessed=8 * inputs.size, transcendentals=0
        ),
        name="back",
    )(left, right, inputs, gain)


def pairs_of(partner):
    found = []
    for y_lo in range(Y_LO):
        for z in range(Z):
            for y_hi in range(Y_HI):
                for x in range(X):
                    for core in range(CORE):
                        ends = ((y_lo, z, y_hi, x, core), partner(y_lo, z, y_hi, x, core))
                        found.append(
                            tuple(
                                ((a % Y_LO) * Z + b % Z) * MP
                                + ((c % Y_HI) * X + d % X) * CORE
                                + e % CORE
                                for a, b, c, d, e in ends
                            )
                        )
    return found


def way(at, core):
    return 1 if (at + core) % 2 == 0 else -1


def swap(values, partner):
    return lax.ppermute(values, AXES, pairs_of(partner))


def by_y_lo(a, b, c, d, e):
    return (1 - a, b, c, d, e)


def by_core(a, b, c, d, e):
    return (a, b, c, d, 1 - e)


def by_z(turn):
    return lambda a, b, c, d, e: (a, b + turn * way(b, e), c, d, e)


def by_x(turn):
    return lambda a, b, c, d, e: (a, b, c, d + turn * way(d, e), e)


def by_y_hi(turn):
    return lambda a, b, c, d, e: (a, b, c + turn * way(c, e), d, e)


def along_z(block):
    first = swap(block, by_z(1))
    second = swap(jnp.concatenate([block, first]), by_z(-1))
    third = swap(second, by_z(1))
    fourth = swap(third, by_z(-1))
    return [block, first, second, third, fourth]


def add(left, right):
    return (left.astype(jnp.float32) + right.astype(jnp.float32)).astype(jnp.bfloat16)


def after(values, earlier):
    return lax.optimization_barrier((values, earlier))[0]


def join(own, got, first):
    return jnp.concatenate([jnp.where(first, own, got), jnp.where(first, got, own)])


def per_device(inputs, ln_gain, w_qkv, q_gain, k_gain, cotangent):
    dp_at, mp_at = lax.axis_index("dp"), lax.axis_index("mp")
    y_lo, z = dp_at // Z, dp_at % Z
    core, x = mp_at % CORE, mp_at // CORE % X
    near, far = (x + 1) // 2 % 2, x // 2
    outer, inner = jnp.where(core == 0, near, far), jnp.where(core == 0, far, near)
    z_way = jnp.where((z + core) % 2 == 0, 1, -1)
    z_places = [(z + z_way * step) % Z for step in Z_STEPS]
    places = jnp.stack(
        [y_lo * Z + at for at in z_places]
        + [(1 - y_lo) * Z + at for at in z_places]
        + [core, outer, inner]
    ).astype(jnp.int32)
    steps = [(at - z) * z_way % Z for at in range(Z)]
    orders = [
        jnp.where(
            step < 2,
            step,
            jnp.where(step < 4, step + 2, jnp.where(step < 6, 11 - step, 9 - step)),
        )
        for step in steps
    ]
    term_places = jnp.stack([Y_LO * order + y for y in range(Y_LO) for order in orders])
    tokens, features = inputs.shape
    rows = tokens // 8
    own_rows = lax.dynamic_slice_in_dim(
        inputs, ((core * 2 + outer) * 2 + inner) * rows, rows, 0
    )
    w_qkv, places, term_places, own_rows, first_core, first_outer, first_inner, first_y = (
        lax.optimization_barrier(
            (
                w_qkv,
                places,
                term_places.astype(jnp.int32),
                own_rows,
                core == 0,
                outer == 0,
                inner == 0,
                y_lo == 0,
            )
        )
    )

    other = swap(w_qkv, by_y_lo)
    blocks = along_z(w_qkv) + along_z(other)
    normed = run_norm(inputs, ln_gain.reshape(1, -1))
    grad_qkv, part, other, sent = run_head(
        places, normed, cotangent, q_gain.reshape(1, -1), k_gain.reshape(1, -1), blocks
    )

    terms = run_terms(term_places, normed, grad_qkv)
    depth = terms.shape[0] // Z
    zero, one, two, three, four = jnp.split(terms, [depth, 2 * depth, 4 * depth, 6 * depth])
    got = swap(sent, by_core)
    rows = part.shape[0]
    other = after(add(other, got[rows:]), terms)
    part = add(part, after(got, other)[:rows])
    got = swap(other, by_x(1))
    across = swap(four, by_z(-1))
    part = add(part, got)
    rows = rows // 2
    part, other = part[:rows], part[rows:]

    three = add(three, after(across, other))
    got = swap(other, by_x(-1))
    across = swap(three, by_z(1))
    part = after(add(part, got), three)

    two = add(two, after(across, part))
    got = swap(part, by_y_hi(1))
    across = swap(two, by_z(-1))
    part = after(add(part, got), two)

    across = after(across, part)
    zero, one = add(zero, across[:depth]), add(one, across[depth:])
    got = swap(part, by_y_hi(-1))
    across = swap(one, by_z(1))
    own = after(run_back(part, got, own_rows, ln_gain.reshape(1, -1)), one)

    zero = add(zero, after(across, own))
    depth = zero.shape[0] // 2
    low, high = zero[:depth], zero[depth:]
    got = swap(own, by_x(-1))
    across = swap(jnp.where(first_y, high, low), by_y_lo)
    own = after(join(own, got, first_inner), zero)

    across = after(across, own).astype(jnp.float32)
    grad_w_qkv = jnp.where(first_y, low, high).astype(jnp.float32) + across
    got = swap(own, by_x(1))
    own = after(join(own, got, first_outer), grad_w_qkv)

    got = swap(own, by_core)
    return (join(own, got, first_core), grad_w_qkv)


def solution(mesh):
    placed = (P("dp", None), P(), P("dp", "mp"), P(), P(), P("dp", "mp"))
    return jax.shard_map(
        per_device,
        mesh=mesh,
        in_specs=placed,
        out_specs=(P("dp", None), P("dp", "mp")),
        check_vma=False,
    )
```

```python
import math

import jax
import jax.numpy as jnp
from jax import lax
from jax.experimental import pallas as pl
from jax.experimental.pallas import tpu as pltpu
from jax.sharding import PartitionSpec as P

EPSILON = 1e-06
Y_LO, Z = 2, 8
Y_HI, X, CORE = 4, 4, 2
MP = Y_HI * X * CORE
AXES = ("dp", "mp")
Z_STEPS = (0, 1, -1, -2, 2, 3, -3, -4)


def normalize(values):
    centred = values - jnp.mean(values, axis=-1, keepdims=True)
    inverse = lax.rsqrt(jnp.mean(centred * centred, axis=-1, keepdims=True) + EPSILON)
    return (centred * inverse, inverse)


def norm_backward(grad_unit, unit_vals, inverse):
    first_mean = jnp.mean(grad_unit, axis=-1, keepdims=True)
    second_mean = jnp.mean(grad_unit * unit_vals, axis=-1, keepdims=True)
    return inverse * (grad_unit - first_mean - unit_vals * second_mean)


def contract(left_op, right_op, left_dim, right_dim):
    return lax.dot_general(
        left_op,
        right_op,
        (((left_dim,), (right_dim,)), ((), ())),
        preferred_element_type=jnp.float32,
    )


def head_grads(qkv_head, cot_head, q_gain, k_gain):
    width = cot_head.shape[1]
    factor = 1.0 / math.sqrt(width)
    q_unit, q_inverse = normalize(qkv_head[:, :width].astype(jnp.float32))
    k_unit, k_inverse = normalize(qkv_head[:, width : 2 * width].astype(jnp.float32))
    values = qkv_head[:, 2 * width :]
    q_normed = (q_unit * q_gain).astype(jnp.bfloat16)
    k_normed = (k_unit * k_gain).astype(jnp.bfloat16)

    def weights_and_grads(rows, columns, row_cot, column_cot, key_axis):
        exp_scores = jnp.exp(contract(rows, columns, 1, 1) * factor)
        attn = exp_scores / jnp.sum(exp_scores, axis=key_axis, keepdims=True)
        grad_attn = contract(row_cot, column_cot, 1, 1)
        centre = jnp.sum(attn * grad_attn, axis=key_axis, keepdims=True)
        return attn, (attn * (grad_attn - centre)).astype(jnp.bfloat16)

    _, grad_scores = weights_and_grads(q_normed, k_normed, cot_head, values, 1)
    attn_t, grad_scores_t = weights_and_grads(k_normed, q_normed, values, cot_head, 0)
    grad_values = contract(attn_t.astype(jnp.bfloat16), cot_head, 1, 0)
    grad_query = norm_backward(
        contract(grad_scores, k_normed, 1, 0) * factor * q_gain, q_unit, q_inverse
    )
    grad_key = norm_backward(
        contract(grad_scores_t, q_normed, 1, 0) * factor * k_gain, k_unit, k_inverse
    )
    return jnp.concatenate([grad_query, grad_key, grad_values], axis=1)


def swap_blocks(rows, outer, inner):
    half = rows.shape[0] // 2
    quarter = half // 2
    rows = jnp.where(outer == 1, jnp.concatenate([rows[half:], rows[:half]]), rows)
    swapped = jnp.concatenate(
        [rows[quarter:half], rows[:quarter], rows[half + quarter :], rows[half : half + quarter]]
    )
    return jnp.where(inner == 1, swapped, rows)


def head_kernel(places, normed, cot, q_gain, k_gain, *refs):
    blocks, refs = refs[:10], refs[10:]
    grad_ref, kept_ref, next_ref, sent_ref, weights = refs
    depth = blocks[0].shape[0]
    y_lo, z, z_way = places[0], places[1], places[2]
    at = 0
    for ref in blocks:
        for part in range(ref.shape[0] // depth):
            y_at = y_lo if at < Z else 1 - y_lo
            to = y_at * Z + lax.rem(z + z_way * Z_STEPS[at % Z] + Z, Z)
            weights[pl.ds(pl.multiple_of(to * depth, depth), depth), :] = ref[
                pl.ds(part * depth, depth), :
            ]
            at += 1
    width = weights.shape[1]
    total = jnp.dot(normed[...], weights[...], preferred_element_type=jnp.float32)
    grads = head_grads(total.astype(jnp.bfloat16), cot[...], q_gain[...], k_gain[...])
    grad_ref[...] = grads.astype(jnp.bfloat16)
    core, outer, inner = places[3], places[4], places[5]
    half = grads.shape[0] // 2
    low, high = grads[:half], grads[half:]
    kept = swap_blocks(jnp.where(core == 0, low, high), outer, inner).astype(jnp.bfloat16)
    sent = swap_blocks(jnp.where(core == 0, high, low), inner, outer).astype(jnp.bfloat16)
    both = jnp.concatenate([sent, kept])
    for first in range(0, weights.shape[0], width):
        at = pl.ds(first, width)
        term = contract(both, weights[at, :], 1, 1).astype(jnp.bfloat16)
        sent_ref[:, at] = term[:half]
        kept_ref[:, at] = term[half : half + half // 2]
        next_ref[:, at] = term[half + half // 2 :]


def run_head(places, normed, cot, q_gain, k_gain, blocks):
    tokens, features = normed.shape
    width = blocks[0].shape[1]
    in_vmem = pl.BlockSpec(memory_space=pltpu.VMEM)
    like = lambda *shape: jax.ShapeDtypeStruct(shape, jnp.bfloat16)
    return pl.pallas_call(
        head_kernel,
        out_shape=(
            like(tokens, width),
            like(tokens // 4, features),
            like(tokens // 4, features),
            like(tokens // 2, features),
        ),
        in_specs=[pl.BlockSpec(memory_space=pltpu.SMEM)] + [in_vmem] * (4 + len(blocks)),
        out_specs=(in_vmem,) * 4,
        scratch_shapes=[
            pltpu.VMEM((features, width), jnp.bfloat16),
        ],
        compiler_params=pltpu.CompilerParams(vmem_limit_bytes=16 * 2**20),
        cost_estimate=pl.CostEstimate(
            flops=3 * tokens * features * width, bytes_accessed=8 * 2**20, transcendentals=200000
        ),
        name="head",
    )(places, normed, cot, q_gain, k_gain, *blocks)


def norm_kernel(inputs, gain, out):
    unit, _ = normalize(inputs[...].astype(jnp.float32))
    out[...] = (unit * gain[...]).astype(out.dtype)


def run_norm(inputs, gain):
    in_vmem = pl.BlockSpec(memory_space=pltpu.VMEM)
    return pl.pallas_call(
        norm_kernel,
        out_shape=jax.ShapeDtypeStruct(inputs.shape, jnp.bfloat16),
        in_specs=[in_vmem, in_vmem],
        out_specs=in_vmem,
        compiler_params=pltpu.CompilerParams(vmem_limit_bytes=12 * 2**20),
        cost_estimate=pl.CostEstimate(
            flops=8 * inputs.size, bytes_accessed=4 * inputs.size, transcendentals=0
        ),
        name="norm",
    )(inputs, gain)


def terms_kernel(places, normed, grads, out):
    features, width = out.shape
    depth = features // (Y_LO * Z)
    z, z_way = places[1], places[2]
    for first in range(0, features, width):
        term = contract(normed[:, pl.ds(first, width)], grads[...], 0, 0).astype(out.dtype)
        for part in range(width // depth):
            y_at, z_at = divmod(first // depth + part, Z)
            step = lax.rem((z_at - z) * z_way + 2 * Z, Z)
            far = jnp.where(step < 4, step + 2, jnp.where(step < 6, 11 - step, 9 - step))
            to = jnp.where(step < 2, step, far) * Y_LO + y_at
            out[pl.ds(pl.multiple_of(to * depth, depth), depth), :] = term[part * depth : (part + 1) * depth]


def run_terms(places, normed, grads):
    tokens, features = normed.shape
    width = grads.shape[1]
    in_vmem = pl.BlockSpec(memory_space=pltpu.VMEM)
    return pl.pallas_call(
        terms_kernel,
        out_shape=jax.ShapeDtypeStruct((features, width), jnp.bfloat16),
        in_specs=[pl.BlockSpec(memory_space=pltpu.SMEM), in_vmem, in_vmem],
        out_specs=in_vmem,
        compiler_params=pltpu.CompilerParams(vmem_limit_bytes=12 * 2**20),
        cost_estimate=pl.CostEstimate(
            flops=2 * tokens * features * width, bytes_accessed=5 * 2**20, transcendentals=0
        ),
        name="terms",
    )(places, normed, grads)


def back_kernel(left, right, inputs, gain, out):
    unit, inverse = normalize(inputs[...].astype(jnp.float32))
    grads = (left[...].astype(jnp.float32) + right[...].astype(jnp.float32)) * gain[...]
    out[...] = norm_backward(grads, unit, inverse).astype(out.dtype)


def run_back(left, right, inputs, gain):
    in_vmem = pl.BlockSpec(memory_space=pltpu.VMEM)
    return pl.pallas_call(
        back_kernel,
        out_shape=jax.ShapeDtypeStruct(inputs.shape, jnp.bfloat16),
        in_specs=[in_vmem] * 4,
        out_specs=in_vmem,
        compiler_params=pltpu.CompilerParams(vmem_limit_bytes=8 * 2**20),
        cost_estimate=pl.CostEstimate(
            flops=20 * inputs.size, bytes_accessed=8 * inputs.size, transcendentals=0
        ),
        name="back",
    )(left, right, inputs, gain)


def pairs_of(partner):
    found = []
    for y_lo in range(Y_LO):
        for z in range(Z):
            for y_hi in range(Y_HI):
                for x in range(X):
                    for core in range(CORE):
                        ends = ((y_lo, z, y_hi, x, core), partner(y_lo, z, y_hi, x, core))
                        found.append(
                            tuple(
                                ((a % Y_LO) * Z + b % Z) * MP
                                + ((c % Y_HI) * X + d % X) * CORE
                                + e % CORE
                                for a, b, c, d, e in ends
                            )
                        )
    return found


def way(at, core):
    return 1 if (at + core) % 2 == 0 else -1


def swap(values, partner):
    return lax.ppermute(values, AXES, pairs_of(partner))


def by_y_lo(a, b, c, d, e):
    return (1 - a, b, c, d, e)


def by_core(a, b, c, d, e):
    return (a, b, c, d, 1 - e)


def by_z(turn):
    return lambda a, b, c, d, e: (a, b + turn * way(b, e), c, d, e)


def by_x(turn):
    return lambda a, b, c, d, e: (a, b, c, d + turn * way(d, e), e)


def by_y_hi(turn):
    return lambda a, b, c, d, e: (a, b, c + turn * way(c, e), d, e)


def along_z(block):
    first = swap(block, by_z(1))
    second = swap(jnp.concatenate([block, first]), by_z(-1))
    third = swap(second, by_z(1))
    fourth = swap(third, by_z(-1))
    return [block, first, second, third, fourth]


def add(left, right):
    return (left.astype(jnp.float32) + right.astype(jnp.float32)).astype(jnp.bfloat16)


def after(values, earlier):
    return lax.optimization_barrier((values, earlier))[0]


def join(own, got, first):
    return jnp.concatenate([jnp.where(first, own, got), jnp.where(first, got, own)])


def per_device(inputs, ln_gain, w_qkv, q_gain, k_gain, cotangent):
    dp_at, mp_at = lax.axis_index("dp"), lax.axis_index("mp")
    y_lo, z = dp_at // Z, dp_at % Z
    core, x = mp_at % CORE, mp_at // CORE % X
    near, far = (x + 1) // 2 % 2, x // 2
    outer, inner = jnp.where(core == 0, near, far), jnp.where(core == 0, far, near)
    z_way = jnp.where((z + core) % 2 == 0, 1, -1)
    places = jnp.stack([y_lo, z, z_way, core, outer, inner]).astype(jnp.int32)
    tokens, features = inputs.shape
    rows = tokens // 8
    own_first = ((core * 2 + outer) * 2 + inner) * rows
    w_qkv, places, own_first, first_core, first_outer, first_inner, first_y = (
        lax.optimization_barrier(
            (
                w_qkv,
                places,
                own_first,
                core == 0,
                outer == 0,
                inner == 0,
                y_lo == 0,
            )
        )
    )

    other = swap(w_qkv, by_y_lo)
    blocks = along_z(w_qkv) + along_z(other)
    normed = run_norm(inputs, ln_gain.reshape(1, -1))
    grad_qkv, part, other, sent = run_head(
        places, normed, cotangent, q_gain.reshape(1, -1), k_gain.reshape(1, -1), blocks
    )

    terms = run_terms(places, normed, grad_qkv)
    depth = terms.shape[0] // Z
    zero, one, two, three, four = jnp.split(terms, [depth, 2 * depth, 4 * depth, 6 * depth])
    got = swap(sent, by_core)
    rows = part.shape[0]
    other = after(add(other, got[rows:]), terms)
    part = add(part, after(got, other)[:rows])
    got = swap(other, by_x(1))
    across = swap(four, by_z(-1))
    part = add(part, got)
    rows = rows // 2
    part, other = part[:rows], part[rows:]

    three = add(three, after(across, other))
    got = swap(other, by_x(-1))
    across = swap(three, by_z(1))
    part = after(add(part, got), three)

    two = add(two, after(across, part))
    got = swap(part, by_y_hi(1))
    across = swap(two, by_z(-1))
    part = after(add(part, got), two)

    across = after(across, part)
    zero, one = add(zero, across[:depth]), add(one, across[depth:])
    got = swap(part, by_y_hi(-1))
    across = swap(one, by_z(1))
    own = lax.dynamic_slice_in_dim(inputs, own_first, rows, 0, allow_negative_indices=False)
    own = after(run_back(part, got, own, ln_gain.reshape(1, -1)), one)

    got = swap(own, by_x(-1))
    own = join(own, got, first_inner)

    zero = add(zero, after(across, own))
    depth = zero.shape[0] // 2
    low, high = zero[:depth], zero[depth:]
    got = swap(own, by_x(1))
    across = swap(jnp.where(first_y, high, low), by_y_lo).astype(jnp.float32)
    grad_w_qkv = jnp.where(first_y, low, high).astype(jnp.float32) + across
    own = after(join(own, got, first_outer), grad_w_qkv)
    return (join(own, swap(own, by_core), first_core), grad_w_qkv)


def solution(mesh):
    placed = (P("dp", None), P(), P("dp", "mp"), P(), P(), P("dp", "mp"))
    return jax.shard_map(
        per_device,
        mesh=mesh,
        in_specs=placed,
        out_specs=(P("dp", None), P("dp", "mp")),
        check_vma=False,
    )
```

```python
import math

import jax
import jax.numpy as jnp
from jax import lax
from jax.experimental import pallas as pl
from jax.experimental.pallas import tpu as pltpu
from jax.sharding import PartitionSpec as P

EPSILON = 1e-06
Y_LO, Z = 2, 8
Y_HI, X, CORE = 4, 4, 2
MP = Y_HI * X * CORE
AXES = ("dp", "mp")
Z_STEPS = (0, 1, -1, -2, 2, 3, -3, -4)


def normalize(values):
    centred = values - jnp.mean(values, axis=-1, keepdims=True)
    inverse = lax.rsqrt(jnp.mean(centred * centred, axis=-1, keepdims=True) + EPSILON)
    return (centred * inverse, inverse)


def norm_backward(grad_unit, unit_vals, inverse):
    first_mean = jnp.mean(grad_unit, axis=-1, keepdims=True)
    second_mean = jnp.mean(grad_unit * unit_vals, axis=-1, keepdims=True)
    return inverse * (grad_unit - first_mean - unit_vals * second_mean)


def contract(left_op, right_op, left_dim, right_dim):
    return lax.dot_general(
        left_op,
        right_op,
        (((left_dim,), (right_dim,)), ((), ())),
        preferred_element_type=jnp.float32,
    )


def head_grads(qkv_head, cot_head, q_gain, k_gain):
    width = cot_head.shape[1]
    factor = 1.0 / math.sqrt(width)
    q_unit, q_inverse = normalize(qkv_head[:, :width].astype(jnp.float32))
    k_unit, k_inverse = normalize(qkv_head[:, width : 2 * width].astype(jnp.float32))
    values = qkv_head[:, 2 * width :]
    q_normed = (q_unit * q_gain).astype(jnp.bfloat16)
    k_normed = (k_unit * k_gain).astype(jnp.bfloat16)

    def weights_and_grads(rows, columns, row_cot, column_cot, key_axis):
        exp_scores = jnp.exp(contract(rows, columns, 1, 1) * factor)
        attn = exp_scores / jnp.sum(exp_scores, axis=key_axis, keepdims=True)
        grad_attn = contract(row_cot, column_cot, 1, 1)
        centre = jnp.sum(attn * grad_attn, axis=key_axis, keepdims=True)
        return attn, (attn * (grad_attn - centre)).astype(jnp.bfloat16)

    _, grad_scores = weights_and_grads(q_normed, k_normed, cot_head, values, 1)
    attn_t, grad_scores_t = weights_and_grads(k_normed, q_normed, values, cot_head, 0)
    grad_values = contract(attn_t.astype(jnp.bfloat16), cot_head, 1, 0)
    grad_query = norm_backward(
        contract(grad_scores, k_normed, 1, 0) * factor * q_gain, q_unit, q_inverse
    )
    grad_key = norm_backward(
        contract(grad_scores_t, q_normed, 1, 0) * factor * k_gain, k_unit, k_inverse
    )
    return jnp.concatenate([grad_query, grad_key, grad_values], axis=1)


def swap_blocks(rows, outer, inner):
    half = rows.shape[0] // 2
    quarter = half // 2
    rows = jnp.where(outer == 1, jnp.concatenate([rows[half:], rows[:half]]), rows)
    swapped = jnp.concatenate(
        [rows[quarter:half], rows[:quarter], rows[half + quarter :], rows[half : half + quarter]]
    )
    return jnp.where(inner == 1, swapped, rows)


def head_kernel(places, normed, cot, q_gain, k_gain, *refs):
    blocks, refs = refs[:10], refs[10:]
    grad_ref, kept_ref, next_ref, sent_ref, weights = refs
    depth = blocks[0].shape[0]
    y_lo, z, z_way = places[0], places[1], places[2]
    at = 0
    for ref in blocks:
        for part in range(ref.shape[0] // depth):
            y_at = y_lo if at < Z else 1 - y_lo
            to = y_at * Z + lax.rem(z + z_way * Z_STEPS[at % Z] + Z, Z)
            weights[pl.ds(pl.multiple_of(to * depth, depth), depth), :] = ref[
                pl.ds(part * depth, depth), :
            ]
            at += 1
    width = weights.shape[1]
    total = jnp.dot(normed[...], weights[...], preferred_element_type=jnp.float32)
    grads = head_grads(total.astype(jnp.bfloat16), cot[...], q_gain[...], k_gain[...])
    grad_ref[...] = grads.astype(jnp.bfloat16)
    core, outer, inner = places[3], places[4], places[5]
    half = grads.shape[0] // 2
    low, high = grads[:half], grads[half:]
    kept = swap_blocks(jnp.where(core == 0, low, high), outer, inner).astype(jnp.bfloat16)
    sent = swap_blocks(jnp.where(core == 0, high, low), inner, outer).astype(jnp.bfloat16)
    both = jnp.concatenate([sent, kept])
    for first in range(0, weights.shape[0], width):
        at = pl.ds(first, width)
        term = contract(both, weights[at, :], 1, 1).astype(jnp.bfloat16)
        sent_ref[:, at] = term[:half]
        kept_ref[:, at] = term[half : half + half // 2]
        next_ref[:, at] = term[half + half // 2 :]


def run_head(places, normed, cot, q_gain, k_gain, blocks):
    tokens, features = normed.shape
    width = blocks[0].shape[1]
    in_vmem = pl.BlockSpec(memory_space=pltpu.VMEM)
    like = lambda *shape: jax.ShapeDtypeStruct(shape, jnp.bfloat16)
    return pl.pallas_call(
        head_kernel,
        out_shape=(
            like(tokens, width),
            like(tokens // 4, features),
            like(tokens // 4, features),
            like(tokens // 2, features),
        ),
        in_specs=[pl.BlockSpec(memory_space=pltpu.SMEM)] + [in_vmem] * (4 + len(blocks)),
        out_specs=(in_vmem,) * 4,
        scratch_shapes=[
            pltpu.VMEM((features, width), jnp.bfloat16),
        ],
        compiler_params=pltpu.CompilerParams(vmem_limit_bytes=16 * 2**20),
        cost_estimate=pl.CostEstimate(
            flops=3 * tokens * features * width, bytes_accessed=8 * 2**20, transcendentals=200000
        ),
        name="head",
    )(places, normed, cot, q_gain, k_gain, *blocks)


def norm_kernel(inputs, gain, out):
    unit, _ = normalize(inputs[...].astype(jnp.float32))
    out[...] = (unit * gain[...]).astype(out.dtype)


def run_norm(inputs, gain):
    in_vmem = pl.BlockSpec(memory_space=pltpu.VMEM)
    return pl.pallas_call(
        norm_kernel,
        out_shape=jax.ShapeDtypeStruct(inputs.shape, jnp.bfloat16),
        in_specs=[in_vmem, in_vmem],
        out_specs=in_vmem,
        compiler_params=pltpu.CompilerParams(vmem_limit_bytes=12 * 2**20),
        cost_estimate=pl.CostEstimate(
            flops=8 * inputs.size, bytes_accessed=4 * inputs.size, transcendentals=0
        ),
        name="norm",
    )(inputs, gain)


def terms_kernel(places, normed, grads, out):
    features, width = out.shape
    depth = features // (Y_LO * Z)
    z, z_way = places[1], places[2]
    for first in range(0, features, width):
        term = contract(normed[:, pl.ds(first, width)], grads[...], 0, 0).astype(out.dtype)
        for part in range(width // depth):
            y_at, z_at = divmod(first // depth + part, Z)
            step = lax.rem((z_at - z) * z_way + 2 * Z, Z)
            far = jnp.where(step < 4, step + 2, jnp.where(step < 6, 11 - step, 9 - step))
            to = jnp.where(step < 2, step, far) * Y_LO + y_at
            out[pl.ds(pl.multiple_of(to * depth, depth), depth), :] = term[part * depth : (part + 1) * depth]


def run_terms(places, normed, grads):
    tokens, features = normed.shape
    width = grads.shape[1]
    in_vmem = pl.BlockSpec(memory_space=pltpu.VMEM)
    return pl.pallas_call(
        terms_kernel,
        out_shape=jax.ShapeDtypeStruct((features, width), jnp.bfloat16),
        in_specs=[pl.BlockSpec(memory_space=pltpu.SMEM), in_vmem, in_vmem],
        out_specs=in_vmem,
        compiler_params=pltpu.CompilerParams(vmem_limit_bytes=12 * 2**20),
        cost_estimate=pl.CostEstimate(
            flops=2 * tokens * features * width, bytes_accessed=5 * 2**20, transcendentals=0
        ),
        name="terms",
    )(places, normed, grads)


def back_kernel(left, right, inputs, gain, out):
    unit, inverse = normalize(inputs[...].astype(jnp.float32))
    grads = (left[...].astype(jnp.float32) + right[...].astype(jnp.float32)) * gain[...]
    out[...] = norm_backward(grads, unit, inverse).astype(out.dtype)


def run_back(left, right, inputs, gain):
    in_vmem = pl.BlockSpec(memory_space=pltpu.VMEM)
    return pl.pallas_call(
        back_kernel,
        out_shape=jax.ShapeDtypeStruct(inputs.shape, jnp.bfloat16),
        in_specs=[in_vmem] * 4,
        out_specs=in_vmem,
        compiler_params=pltpu.CompilerParams(vmem_limit_bytes=8 * 2**20),
        cost_estimate=pl.CostEstimate(
            flops=20 * inputs.size, bytes_accessed=8 * inputs.size, transcendentals=0
        ),
        name="back",
    )(left, right, inputs, gain)


def pairs_of(partner):
    found = []
    for y_lo in range(Y_LO):
        for z in range(Z):
            for y_hi in range(Y_HI):
                for x in range(X):
                    for core in range(CORE):
                        ends = ((y_lo, z, y_hi, x, core), partner(y_lo, z, y_hi, x, core))
                        found.append(
                            tuple(
                                ((a % Y_LO) * Z + b % Z) * MP
                                + ((c % Y_HI) * X + d % X) * CORE
                                + e % CORE
                                for a, b, c, d, e in ends
                            )
                        )
    return found


def way(at, core):
    return 1 if (at + core) % 2 == 0 else -1


def swap(values, partner):
    return lax.ppermute(values, AXES, pairs_of(partner))


def by_y_lo(a, b, c, d, e):
    return (1 - a, b, c, d, e)


def by_core(a, b, c, d, e):
    return (a, b, c, d, 1 - e)


def by_z(turn):
    return lambda a, b, c, d, e: (a, b + turn * way(b, e), c, d, e)


def by_x(turn):
    return lambda a, b, c, d, e: (a, b, c, d + turn * way(d, e), e)


def by_y_hi(turn):
    return lambda a, b, c, d, e: (a, b, c + turn * way(c, e), d, e)


def along_z(block):
    first = swap(block, by_z(1))
    second = swap(jnp.concatenate([block, first]), by_z(-1))
    third = swap(second, by_z(1))
    fourth = swap(third, by_z(-1))
    return [block, first, second, third, fourth]


def add(left, right):
    return (left.astype(jnp.float32) + right.astype(jnp.float32)).astype(jnp.bfloat16)


def after(values, earlier):
    return lax.optimization_barrier((values, earlier))[0]


def join(own, got, first):
    return jnp.concatenate([jnp.where(first, own, got), jnp.where(first, got, own)])


def per_device(inputs, ln_gain, w_qkv, q_gain, k_gain, cotangent):
    dp_at, mp_at = lax.axis_index("dp"), lax.axis_index("mp")
    y_lo, z = dp_at // Z, dp_at % Z
    core, x = mp_at % CORE, mp_at // CORE % X
    near, far = (x + 1) // 2 % 2, x // 2
    outer, inner = jnp.where(core == 0, near, far), jnp.where(core == 0, far, near)
    z_way = jnp.where((z + core) % 2 == 0, 1, -1)
    places = jnp.stack([y_lo, z, z_way, core, outer, inner]).astype(jnp.int32)
    tokens, features = inputs.shape
    rows = tokens // 8
    own_first = ((core * 2 + outer) * 2 + inner) * rows
    w_qkv, places, own_first, first_core, first_outer, first_inner, first_y = (
        lax.optimization_barrier(
            (
                w_qkv,
                places,
                own_first,
                core == 0,
                outer == 0,
                inner == 0,
                y_lo == 0,
            )
        )
    )

    other = swap(w_qkv, by_y_lo)
    blocks = along_z(w_qkv) + along_z(other)
    normed = run_norm(inputs, ln_gain.reshape(1, -1))
    grad_qkv, part, other, sent = run_head(
        places, normed, cotangent, q_gain.reshape(1, -1), k_gain.reshape(1, -1), blocks
    )

    terms = run_terms(places, normed, grad_qkv)
    depth = terms.shape[0] // Z
    zero, one, two, three, four = jnp.split(terms, [depth, 2 * depth, 4 * depth, 6 * depth])
    got = swap(sent, by_core)
    rows = part.shape[0]
    other = after(add(other, got[rows:]), terms)
    part = add(part, after(got, other)[:rows])
    got = swap(other, by_x(1))
    across = swap(four, by_z(-1))
    part = add(part, got)
    rows = rows // 2
    part, other = part[:rows], part[rows:]

    three = add(three, after(across, other))
    got = swap(other, by_x(-1))
    across = swap(three, by_z(1))
    part = after(add(part, got), three)

    two = add(two, after(across, part))
    got = swap(part, by_y_hi(1))
    across = swap(two, by_z(-1))
    part = after(add(part, got), two)

    across = after(across, part)
    zero, one = add(zero, across[:depth]), add(one, across[depth:])
    got = swap(part, by_y_hi(-1))
    across = swap(one, by_z(1))
    own = lax.dynamic_slice_in_dim(inputs, own_first, rows, 0, allow_negative_indices=False)
    own = after(run_back(part, got, own, ln_gain.reshape(1, -1)), one)

    got = swap(own, by_x(-1))
    own = join(own, got, first_inner)

    zero = add(zero, after(across, own))
    depth = zero.shape[0] // 2
    low, high = zero[:depth], zero[depth:]
    got = swap(own, by_x(1))
    across = swap(jnp.where(first_y, high, low), by_y_lo)
    own = after(join(own, got, first_outer), across)
    got = swap(own, by_core)
    grad_w_qkv = jnp.where(first_y, low, high).astype(jnp.float32) + across.astype(jnp.float32)
    return (join(own, got, first_core), grad_w_qkv)


def solution(mesh):
    placed = (P("dp", None), P(), P("dp", "mp"), P(), P(), P("dp", "mp"))
    return jax.shard_map(
        per_device,
        mesh=mesh,
        in_specs=placed,
        out_specs=(P("dp", None), P("dp", "mp")),
        check_vma=False,
    )
```

```python
import math

import jax
import jax.numpy as jnp
from jax import lax
from jax.experimental import pallas as pl
from jax.experimental.pallas import tpu as pltpu
from jax.sharding import PartitionSpec as P

EPSILON = 1e-06
Y_LO, Z = 2, 8
Y_HI, X, CORE = 4, 4, 2
MP = Y_HI * X * CORE
AXES = ("dp", "mp")
Z_STEPS = (0, 1, -1, -2, 2, 3, -3, -4)


def normalize(values):
    centred = values - jnp.mean(values, axis=-1, keepdims=True)
    inverse = lax.rsqrt(jnp.mean(centred * centred, axis=-1, keepdims=True) + EPSILON)
    return (centred * inverse, inverse)


def norm_backward(grad_unit, unit_vals, inverse):
    first_mean = jnp.mean(grad_unit, axis=-1, keepdims=True)
    second_mean = jnp.mean(grad_unit * unit_vals, axis=-1, keepdims=True)
    return inverse * (grad_unit - first_mean - unit_vals * second_mean)


def contract(left_op, right_op, left_dim, right_dim):
    return lax.dot_general(
        left_op,
        right_op,
        (((left_dim,), (right_dim,)), ((), ())),
        preferred_element_type=jnp.float32,
    )


def head_grads(qkv_head, cot_head, q_gain, k_gain):
    width = cot_head.shape[1]
    factor = 1.0 / math.sqrt(width)
    q_unit, q_inverse = normalize(qkv_head[:, :width].astype(jnp.float32))
    k_unit, k_inverse = normalize(qkv_head[:, width : 2 * width].astype(jnp.float32))
    values = qkv_head[:, 2 * width :]
    q_normed = (q_unit * q_gain).astype(jnp.bfloat16)
    k_normed = (k_unit * k_gain).astype(jnp.bfloat16)

    def weights_and_grads(rows, columns, row_cot, column_cot, key_axis):
        exp_scores = jnp.exp(contract(rows, columns, 1, 1) * factor)
        attn = exp_scores / jnp.sum(exp_scores, axis=key_axis, keepdims=True)
        grad_attn = contract(row_cot, column_cot, 1, 1)
        centre = jnp.sum(attn * grad_attn, axis=key_axis, keepdims=True)
        return attn, (attn * (grad_attn - centre)).astype(jnp.bfloat16)

    _, grad_scores = weights_and_grads(q_normed, k_normed, cot_head, values, 1)
    attn_t, grad_scores_t = weights_and_grads(k_normed, q_normed, values, cot_head, 0)
    grad_values = contract(attn_t.astype(jnp.bfloat16), cot_head, 1, 0)
    grad_query = norm_backward(
        contract(grad_scores, k_normed, 1, 0) * factor * q_gain, q_unit, q_inverse
    )
    grad_key = norm_backward(
        contract(grad_scores_t, q_normed, 1, 0) * factor * k_gain, k_unit, k_inverse
    )
    return jnp.concatenate([grad_query, grad_key, grad_values], axis=1)


def swap_blocks(rows, outer, inner):
    half = rows.shape[0] // 2
    quarter = half // 2
    rows = jnp.where(outer == 1, jnp.concatenate([rows[half:], rows[:half]]), rows)
    swapped = jnp.concatenate(
        [rows[quarter:half], rows[:quarter], rows[half + quarter :], rows[half : half + quarter]]
    )
    return jnp.where(inner == 1, swapped, rows)


def head_kernel(places, normed, cot, q_gain, k_gain, *refs):
    blocks, refs = refs[:10], refs[10:]
    grad_ref, kept_ref, next_ref, sent_ref, weights = refs
    depth = blocks[0].shape[0]
    y_lo, z, z_way = places[0], places[1], places[2]
    at = 0
    for ref in blocks:
        for part in range(ref.shape[0] // depth):
            y_at = y_lo if at < Z else 1 - y_lo
            to = y_at * Z + lax.rem(z + z_way * Z_STEPS[at % Z] + Z, Z)
            weights[pl.ds(pl.multiple_of(to * depth, depth), depth), :] = ref[
                pl.ds(part * depth, depth), :
            ]
            at += 1
    width = weights.shape[1]
    total = jnp.dot(normed[...], weights[...], preferred_element_type=jnp.float32)
    grads = head_grads(total.astype(jnp.bfloat16), cot[...], q_gain[...], k_gain[...])
    grad_ref[...] = grads.astype(jnp.bfloat16)
    core, outer, inner = places[3], places[4], places[5]
    half = grads.shape[0] // 2
    low, high = grads[:half], grads[half:]
    kept = swap_blocks(jnp.where(core == 0, low, high), outer, inner).astype(jnp.bfloat16)
    sent = swap_blocks(jnp.where(core == 0, high, low), inner, outer).astype(jnp.bfloat16)
    both = jnp.concatenate([sent, kept])
    for first in range(0, weights.shape[0], width):
        at = pl.ds(first, width)
        term = contract(both, weights[at, :], 1, 1).astype(jnp.bfloat16)
        sent_ref[:, at] = term[:half]
        kept_ref[:, at] = term[half : half + half // 2]
        next_ref[:, at] = term[half + half // 2 :]


def run_head(places, normed, cot, q_gain, k_gain, blocks):
    tokens, features = normed.shape
    width = blocks[0].shape[1]
    in_vmem = pl.BlockSpec(memory_space=pltpu.VMEM)
    like = lambda *shape: jax.ShapeDtypeStruct(shape, jnp.bfloat16)
    return pl.pallas_call(
        head_kernel,
        out_shape=(
            like(tokens, width),
            like(tokens // 4, features),
            like(tokens // 4, features),
            like(tokens // 2, features),
        ),
        in_specs=[pl.BlockSpec(memory_space=pltpu.SMEM)] + [in_vmem] * (4 + len(blocks)),
        out_specs=(in_vmem,) * 4,
        scratch_shapes=[
            pltpu.VMEM((features, width), jnp.bfloat16),
        ],
        compiler_params=pltpu.CompilerParams(vmem_limit_bytes=16 * 2**20),
        cost_estimate=pl.CostEstimate(
            flops=3 * tokens * features * width, bytes_accessed=8 * 2**20, transcendentals=200000
        ),
        name="head",
    )(places, normed, cot, q_gain, k_gain, *blocks)


def norm_kernel(inputs, gain, out):
    unit, _ = normalize(inputs[...].astype(jnp.float32))
    out[...] = (unit * gain[...]).astype(out.dtype)


def run_norm(inputs, gain):
    in_vmem = pl.BlockSpec(memory_space=pltpu.VMEM)
    return pl.pallas_call(
        norm_kernel,
        out_shape=jax.ShapeDtypeStruct(inputs.shape, jnp.bfloat16),
        in_specs=[in_vmem, in_vmem],
        out_specs=in_vmem,
        compiler_params=pltpu.CompilerParams(vmem_limit_bytes=12 * 2**20),
        cost_estimate=pl.CostEstimate(
            flops=8 * inputs.size, bytes_accessed=4 * inputs.size, transcendentals=0
        ),
        name="norm",
    )(inputs, gain)


def terms_kernel(places, normed, grads, out):
    features, width = out.shape
    depth = features // (Y_LO * Z)
    z, z_way = places[1], places[2]
    for first in range(0, features, width):
        term = contract(normed[:, pl.ds(first, width)], grads[...], 0, 0).astype(out.dtype)
        for part in range(width // depth):
            y_at, z_at = divmod(first // depth + part, Z)
            step = lax.rem((z_at - z) * z_way + 2 * Z, Z)
            far = jnp.where(step < 4, step + 2, jnp.where(step < 6, 11 - step, 9 - step))
            to = jnp.where(step < 2, step, far) * Y_LO + y_at
            out[pl.ds(pl.multiple_of(to * depth, depth), depth), :] = term[part * depth : (part + 1) * depth]


def run_terms(places, normed, grads):
    tokens, features = normed.shape
    width = grads.shape[1]
    in_vmem = pl.BlockSpec(memory_space=pltpu.VMEM)
    return pl.pallas_call(
        terms_kernel,
        out_shape=jax.ShapeDtypeStruct((features, width), jnp.bfloat16),
        in_specs=[pl.BlockSpec(memory_space=pltpu.SMEM), in_vmem, in_vmem],
        out_specs=in_vmem,
        compiler_params=pltpu.CompilerParams(vmem_limit_bytes=12 * 2**20),
        cost_estimate=pl.CostEstimate(
            flops=2 * tokens * features * width, bytes_accessed=5 * 2**20, transcendentals=0
        ),
        name="terms",
    )(places, normed, grads)


def back_kernel(left, right, inputs, gain, out):
    unit, inverse = normalize(inputs[...].astype(jnp.float32))
    grads = (left[...].astype(jnp.float32) + right[...].astype(jnp.float32)) * gain[...]
    out[...] = norm_backward(grads, unit, inverse).astype(out.dtype)


def run_back(left, right, inputs, gain):
    in_vmem = pl.BlockSpec(memory_space=pltpu.VMEM)
    return pl.pallas_call(
        back_kernel,
        out_shape=jax.ShapeDtypeStruct(inputs.shape, jnp.bfloat16),
        in_specs=[in_vmem] * 4,
        out_specs=in_vmem,
        compiler_params=pltpu.CompilerParams(vmem_limit_bytes=8 * 2**20),
        cost_estimate=pl.CostEstimate(
            flops=20 * inputs.size, bytes_accessed=8 * inputs.size, transcendentals=0
        ),
        name="back",
    )(left, right, inputs, gain)


def pairs_of(partner):
    found = []
    for y_lo in range(Y_LO):
        for z in range(Z):
            for y_hi in range(Y_HI):
                for x in range(X):
                    for core in range(CORE):
                        ends = ((y_lo, z, y_hi, x, core), partner(y_lo, z, y_hi, x, core))
                        found.append(
                            tuple(
                                ((a % Y_LO) * Z + b % Z) * MP
                                + ((c % Y_HI) * X + d % X) * CORE
                                + e % CORE
                                for a, b, c, d, e in ends
                            )
                        )
    return found


def way(at, core):
    return 1 if (at + core) % 2 == 0 else -1


def swap(values, partner):
    return lax.ppermute(values, AXES, pairs_of(partner))


def by_y_lo(a, b, c, d, e):
    return (1 - a, b, c, d, e)


def by_core(a, b, c, d, e):
    return (a, b, c, d, 1 - e)


def by_z(turn):
    return lambda a, b, c, d, e: (a, b + turn * way(b, e), c, d, e)


def by_x(turn):
    return lambda a, b, c, d, e: (a, b, c, d + turn * way(d, e), e)


def by_y_hi(turn):
    return lambda a, b, c, d, e: (a, b, c + turn * way(c, e), d, e)


def along_z(block):
    first = swap(block, by_z(1))
    second = swap(jnp.concatenate([block, first]), by_z(-1))
    third = swap(second, by_z(1))
    fourth = swap(third, by_z(-1))
    return [block, first, second, third, fourth]


def add(left, right):
    return (left.astype(jnp.float32) + right.astype(jnp.float32)).astype(jnp.bfloat16)


def after(values, earlier):
    return lax.optimization_barrier((values, earlier))[0]


def join(own, got, first):
    return jnp.concatenate([jnp.where(first, own, got), jnp.where(first, got, own)])


def per_device(inputs, ln_gain, w_qkv, q_gain, k_gain, cotangent):
    dp_at, mp_at = lax.axis_index("dp"), lax.axis_index("mp")
    y_lo, z = dp_at // Z, dp_at % Z
    core, x = mp_at % CORE, mp_at // CORE % X
    near, far = (x + 1) // 2 % 2, x // 2
    outer, inner = jnp.where(core == 0, near, far), jnp.where(core == 0, far, near)
    z_way = jnp.where((z + core) % 2 == 0, 1, -1)
    places = jnp.stack([y_lo, z, z_way, core, outer, inner]).astype(jnp.int32)
    tokens, features = inputs.shape
    rows = tokens // 8
    own_first = ((core * 2 + outer) * 2 + inner) * rows
    w_qkv, places, own_first, first_core, first_outer, first_inner, first_y = (
        lax.optimization_barrier(
            (
                w_qkv,
                places,
                own_first,
                core == 0,
                outer == 0,
                inner == 0,
                y_lo == 0,
            )
        )
    )

    later = [pair for pair in pairs_of(by_y_lo) if pair[0] % CORE == 1]
    got_gain = lax.ppermute(q_gain, AXES, later)
    w_qkv, got_gain = lax.optimization_barrier((w_qkv, got_gain))
    q_gain = jnp.where(first_core, q_gain, got_gain)
    other = swap(w_qkv, by_y_lo)
    blocks = along_z(w_qkv) + along_z(other)
    normed = run_norm(inputs, ln_gain.reshape(1, -1))
    grad_qkv, part, other, sent = run_head(
        places, normed, cotangent, q_gain.reshape(1, -1), k_gain.reshape(1, -1), blocks
    )

    terms = run_terms(places, normed, grad_qkv)
    depth = terms.shape[0] // Z
    zero, one, two, three, four = jnp.split(terms, [depth, 2 * depth, 4 * depth, 6 * depth])
    got = swap(sent, by_core)
    rows = part.shape[0]
    other = after(add(other, got[rows:]), terms)
    part = add(part, after(got, other)[:rows])
    got = swap(other, by_x(1))
    across = swap(four, by_z(-1))
    part = add(part, got)
    rows = rows // 2
    part, other = part[:rows], part[rows:]

    three = add(three, after(across, other))
    got = swap(other, by_x(-1))
    across = swap(three, by_z(1))
    part = after(add(part, got), three)

    two = add(two, after(across, part))
    got = swap(part, by_y_hi(1))
    across = swap(two, by_z(-1))
    part = after(add(part, got), two)

    across = after(across, part)
    zero, one = add(zero, across[:depth]), add(one, across[depth:])
    got = swap(part, by_y_hi(-1))
    across = swap(one, by_z(1))
    own = lax.dynamic_slice_in_dim(inputs, own_first, rows, 0, allow_negative_indices=False)
    own = after(run_back(part, got, own, ln_gain.reshape(1, -1)), one)

    got = swap(own, by_x(-1))
    own = join(own, got, first_inner)

    zero = add(zero, after(across, own))
    depth = zero.shape[0] // 2
    low, high = zero[:depth], zero[depth:]
    got = swap(own, by_x(1))
    across = swap(jnp.where(first_y, high, low), by_y_lo)
    own = after(join(own, got, first_outer), across)
    got = swap(own, by_core)
    grad_w_qkv = jnp.where(first_y, low, high).astype(jnp.float32) + across.astype(jnp.float32)
    return (join(own, got, first_core), grad_w_qkv)


def solution(mesh):
    placed = (P("dp", None), P(), P("dp", "mp"), P(), P(), P("dp", "mp"))
    return jax.shard_map(
        per_device,
        mesh=mesh,
        in_specs=placed,
        out_specs=(P("dp", None), P("dp", "mp")),
        check_vma=False,
    )
```

```python
import math

import jax
import jax.numpy as jnp
from jax import lax
from jax.experimental import pallas as pl
from jax.experimental.pallas import tpu as pltpu
from jax.sharding import PartitionSpec as P

EPSILON = 1e-06
Y_LO, Z = 2, 8
Y_HI, X, CORE = 4, 4, 2
MP = Y_HI * X * CORE
AXES = ("dp", "mp")
Z_STEPS = (0, 1, -1, -2, 2, 3, -3, -4)


def normalize(values):
    centred = values - jnp.mean(values, axis=-1, keepdims=True)
    inverse = lax.rsqrt(jnp.mean(centred * centred, axis=-1, keepdims=True) + EPSILON)
    return (centred * inverse, inverse)


def norm_backward(grad_unit, unit_vals, inverse):
    first_mean = jnp.mean(grad_unit, axis=-1, keepdims=True)
    second_mean = jnp.mean(grad_unit * unit_vals, axis=-1, keepdims=True)
    return inverse * (grad_unit - first_mean - unit_vals * second_mean)


def contract(left_op, right_op, left_dim, right_dim):
    return lax.dot_general(
        left_op,
        right_op,
        (((left_dim,), (right_dim,)), ((), ())),
        preferred_element_type=jnp.float32,
    )


def head_grads(qkv_head, cot_head, q_gain, k_gain):
    width = cot_head.shape[1]
    factor = 1.0 / math.sqrt(width)
    q_unit, q_inverse = normalize(qkv_head[:, :width].astype(jnp.float32))
    k_unit, k_inverse = normalize(qkv_head[:, width : 2 * width].astype(jnp.float32))
    values = qkv_head[:, 2 * width :]
    q_normed = (q_unit * q_gain).astype(jnp.bfloat16)
    k_normed = (k_unit * k_gain).astype(jnp.bfloat16)

    def weights_and_grads(rows, columns, row_cot, column_cot, key_axis):
        exp_scores = jnp.exp(contract(rows, columns, 1, 1) * factor)
        attn = exp_scores / jnp.sum(exp_scores, axis=key_axis, keepdims=True)
        grad_attn = contract(row_cot, column_cot, 1, 1)
        centre = jnp.sum(attn * grad_attn, axis=key_axis, keepdims=True)
        return attn, (attn * (grad_attn - centre)).astype(jnp.bfloat16)

    _, grad_scores = weights_and_grads(q_normed, k_normed, cot_head, values, 1)
    attn_t, grad_scores_t = weights_and_grads(k_normed, q_normed, values, cot_head, 0)
    grad_values = contract(attn_t.astype(jnp.bfloat16), cot_head, 1, 0)
    grad_query = norm_backward(
        contract(grad_scores, k_normed, 1, 0) * factor * q_gain, q_unit, q_inverse
    )
    grad_key = norm_backward(
        contract(grad_scores_t, q_normed, 1, 0) * factor * k_gain, k_unit, k_inverse
    )
    return jnp.concatenate([grad_query, grad_key, grad_values], axis=1)


def swap_blocks(rows, outer, inner):
    half = rows.shape[0] // 2
    quarter = half // 2
    rows = jnp.where(outer == 1, jnp.concatenate([rows[half:], rows[:half]]), rows)
    swapped = jnp.concatenate(
        [rows[quarter:half], rows[:quarter], rows[half + quarter :], rows[half : half + quarter]]
    )
    return jnp.where(inner == 1, swapped, rows)


def head_kernel(places, normed, cot, q_gain, k_gain, *refs):
    blocks, refs = refs[:10], refs[10:]
    grad_ref, kept_ref, next_ref, sent_ref, weights = refs
    depth = blocks[0].shape[0]
    y_lo, z, z_way = places[0], places[1], places[2]
    at = 0
    for ref in blocks:
        for part in range(ref.shape[0] // depth):
            y_at = y_lo if at < Z else 1 - y_lo
            to = y_at * Z + lax.rem(z + z_way * Z_STEPS[at % Z] + Z, Z)
            weights[pl.ds(pl.multiple_of(to * depth, depth), depth), :] = ref[
                pl.ds(part * depth, depth), :
            ]
            at += 1
    width = weights.shape[1]
    total = jnp.dot(normed[...], weights[...], preferred_element_type=jnp.float32)
    grads = head_grads(total.astype(jnp.bfloat16), cot[...], q_gain[...], k_gain[...])
    grad_ref[...] = grads.astype(jnp.bfloat16)
    core, outer, inner = places[3], places[4], places[5]
    half = grads.shape[0] // 2
    low, high = grads[:half], grads[half:]
    kept = swap_blocks(jnp.where(core == 0, low, high), outer, inner).astype(jnp.bfloat16)
    sent = swap_blocks(jnp.where(core == 0, high, low), inner, outer).astype(jnp.bfloat16)
    both = jnp.concatenate([sent, kept])
    for first in range(0, weights.shape[0], width):
        at = pl.ds(first, width)
        term = contract(both, weights[at, :], 1, 1).astype(jnp.bfloat16)
        sent_ref[:, at] = term[:half]
        kept_ref[:, at] = term[half : half + half // 2]
        next_ref[:, at] = term[half + half // 2 :]


def run_head(places, normed, cot, q_gain, k_gain, blocks):
    tokens, features = normed.shape
    width = blocks[0].shape[1]
    in_vmem = pl.BlockSpec(memory_space=pltpu.VMEM)
    like = lambda *shape: jax.ShapeDtypeStruct(shape, jnp.bfloat16)
    return pl.pallas_call(
        head_kernel,
        out_shape=(
            like(tokens, width),
            like(tokens // 4, features),
            like(tokens // 4, features),
            like(tokens // 2, features),
        ),
        in_specs=[pl.BlockSpec(memory_space=pltpu.SMEM)] + [in_vmem] * (4 + len(blocks)),
        out_specs=(in_vmem,) * 4,
        scratch_shapes=[
            pltpu.VMEM((features, width), jnp.bfloat16),
        ],
        compiler_params=pltpu.CompilerParams(vmem_limit_bytes=16 * 2**20),
        cost_estimate=pl.CostEstimate(
            flops=3 * tokens * features * width, bytes_accessed=8 * 2**20, transcendentals=200000
        ),
        name="head",
    )(places, normed, cot, q_gain, k_gain, *blocks)


def norm_kernel(inputs, gain, out):
    unit, _ = normalize(inputs[...].astype(jnp.float32))
    out[...] = (unit * gain[...]).astype(out.dtype)


def run_norm(inputs, gain):
    in_vmem = pl.BlockSpec(memory_space=pltpu.VMEM)
    return pl.pallas_call(
        norm_kernel,
        out_shape=jax.ShapeDtypeStruct(inputs.shape, jnp.bfloat16),
        in_specs=[in_vmem, in_vmem],
        out_specs=in_vmem,
        compiler_params=pltpu.CompilerParams(vmem_limit_bytes=12 * 2**20),
        cost_estimate=pl.CostEstimate(
            flops=8 * inputs.size, bytes_accessed=4 * inputs.size, transcendentals=0
        ),
        name="norm",
    )(inputs, gain)


def terms_kernel(places, normed, grads, out):
    features, width = out.shape
    depth = features // (Y_LO * Z)
    z, z_way = places[1], places[2]
    for first in range(0, features, width):
        term = contract(normed[:, pl.ds(first, width)], grads[...], 0, 0).astype(out.dtype)
        for part in range(width // depth):
            y_at, z_at = divmod(first // depth + part, Z)
            step = lax.rem((z_at - z) * z_way + 2 * Z, Z)
            far = jnp.where(step < 4, step + 2, jnp.where(step < 6, 11 - step, 9 - step))
            to = jnp.where(step < 2, step, far) * Y_LO + y_at
            out[pl.ds(pl.multiple_of(to * depth, depth), depth), :] = term[part * depth : (part + 1) * depth]


def run_terms(places, normed, grads):
    tokens, features = normed.shape
    width = grads.shape[1]
    in_vmem = pl.BlockSpec(memory_space=pltpu.VMEM)
    return pl.pallas_call(
        terms_kernel,
        out_shape=jax.ShapeDtypeStruct((features, width), jnp.bfloat16),
        in_specs=[pl.BlockSpec(memory_space=pltpu.SMEM), in_vmem, in_vmem],
        out_specs=in_vmem,
        compiler_params=pltpu.CompilerParams(vmem_limit_bytes=12 * 2**20),
        cost_estimate=pl.CostEstimate(
            flops=2 * tokens * features * width, bytes_accessed=5 * 2**20, transcendentals=0
        ),
        name="terms",
    )(places, normed, grads)


def back_kernel(left, right, inputs, gain, out):
    unit, inverse = normalize(inputs[...].astype(jnp.float32))
    grads = (left[...].astype(jnp.float32) + right[...].astype(jnp.float32)) * gain[...]
    out[...] = norm_backward(grads, unit, inverse).astype(out.dtype)


def run_back(left, right, inputs, gain):
    in_vmem = pl.BlockSpec(memory_space=pltpu.VMEM)
    return pl.pallas_call(
        back_kernel,
        out_shape=jax.ShapeDtypeStruct(inputs.shape, jnp.bfloat16),
        in_specs=[in_vmem] * 4,
        out_specs=in_vmem,
        compiler_params=pltpu.CompilerParams(vmem_limit_bytes=8 * 2**20),
        cost_estimate=pl.CostEstimate(
            flops=20 * inputs.size, bytes_accessed=8 * inputs.size, transcendentals=0
        ),
        name="back",
    )(left, right, inputs, gain)


def pairs_of(partner):
    found = []
    for y_lo in range(Y_LO):
        for z in range(Z):
            for y_hi in range(Y_HI):
                for x in range(X):
                    for core in range(CORE):
                        ends = ((y_lo, z, y_hi, x, core), partner(y_lo, z, y_hi, x, core))
                        found.append(
                            tuple(
                                ((a % Y_LO) * Z + b % Z) * MP
                                + ((c % Y_HI) * X + d % X) * CORE
                                + e % CORE
                                for a, b, c, d, e in ends
                            )
                        )
    return found


def way(at, core):
    return 1 if (at + core) % 2 == 0 else -1


def swap(values, partner):
    return lax.ppermute(values, AXES, pairs_of(partner))


def by_y_lo(a, b, c, d, e):
    return (1 - a, b, c, d, e)


def by_core(a, b, c, d, e):
    return (a, b, c, d, 1 - e)


def by_z(turn):
    return lambda a, b, c, d, e: (a, b + turn * way(b, e), c, d, e)


def by_x(turn):
    return lambda a, b, c, d, e: (a, b, c, d + turn * way(d, e), e)


def by_y_hi(turn):
    return lambda a, b, c, d, e: (a, b, c + turn * way(c, e), d, e)


def along_z(block):
    first = swap(block, by_z(1))
    second = swap(jnp.concatenate([block, first]), by_z(-1))
    third = swap(second, by_z(1))
    fourth = swap(third, by_z(-1))
    return [block, first, second, third, fourth]


def add(left, right):
    return (left.astype(jnp.float32) + right.astype(jnp.float32)).astype(jnp.bfloat16)


def after(values, earlier):
    return lax.optimization_barrier((values, earlier))[0]


def join(own, got, first):
    return jnp.concatenate([jnp.where(first, own, got), jnp.where(first, got, own)])


def per_device(inputs, ln_gain, w_qkv, q_gain, k_gain, cotangent):
    dp_at, mp_at = lax.axis_index("dp"), lax.axis_index("mp")
    y_lo, z = dp_at // Z, dp_at % Z
    core, x = mp_at % CORE, mp_at // CORE % X
    near, far = (x + 1) // 2 % 2, x // 2
    outer, inner = jnp.where(core == 0, near, far), jnp.where(core == 0, far, near)
    z_way = jnp.where((z + core) % 2 == 0, 1, -1)
    places = jnp.stack([y_lo, z, z_way, core, outer, inner]).astype(jnp.int32)
    tokens, features = inputs.shape
    rows = tokens // 8
    own_first = ((core * 2 + outer) * 2 + inner) * rows
    w_qkv, places, own_first, first_core, first_outer, first_inner, first_y = (
        lax.optimization_barrier(
            (
                w_qkv,
                places,
                own_first,
                core == 0,
                outer == 0,
                inner == 0,
                y_lo == 0,
            )
        )
    )

    later = [pair for pair in pairs_of(by_y_lo) if pair[0] % CORE == 1]
    got_gain = lax.ppermute(q_gain, AXES, later)
    w_qkv, got_gain = lax.optimization_barrier((w_qkv, got_gain))
    q_gain = jnp.where(first_core, q_gain, got_gain)
    other = swap(w_qkv, by_y_lo)
    blocks = along_z(w_qkv) + along_z(other)
    normed = run_norm(inputs, ln_gain.reshape(1, -1))
    grad_qkv, part, other, sent = run_head(
        places, normed, cotangent, q_gain.reshape(1, -1), k_gain.reshape(1, -1), blocks
    )

    terms = run_terms(places, normed, grad_qkv)
    depth = terms.shape[0] // Z
    zero, one, two, three, four = jnp.split(terms, [depth, 2 * depth, 4 * depth, 6 * depth])
    got = swap(sent, by_core)
    rows = part.shape[0]
    got_gain = lax.ppermute(after(ln_gain, terms), AXES, later)
    other = after(add(other, got[rows:]), terms)
    other, got_gain = lax.optimization_barrier((other, got_gain))
    ln_gain = jnp.where(first_core, ln_gain, got_gain)
    part = add(part, after(got, other)[:rows])
    got = swap(other, by_x(1))
    across = swap(four, by_z(-1))
    part = add(part, got)
    rows = rows // 2
    part, other = part[:rows], part[rows:]

    three = add(three, after(across, other))
    got = swap(other, by_x(-1))
    across = swap(three, by_z(1))
    part = after(add(part, got), three)

    two = add(two, after(across, part))
    got = swap(part, by_y_hi(1))
    across = swap(two, by_z(-1))
    part = after(add(part, got), two)

    across = after(across, part)
    zero, one = add(zero, across[:depth]), add(one, across[depth:])
    got = swap(part, by_y_hi(-1))
    across = swap(one, by_z(1))
    own = lax.dynamic_slice_in_dim(inputs, own_first, rows, 0, allow_negative_indices=False)
    own = after(run_back(part, got, own, ln_gain.reshape(1, -1)), one)

    got = swap(own, by_x(-1))
    own = join(own, got, first_inner)

    zero = add(zero, after(across, own))
    depth = zero.shape[0] // 2
    low, high = zero[:depth], zero[depth:]
    got = swap(own, by_x(1))
    across = swap(jnp.where(first_y, high, low), by_y_lo)
    own = after(join(own, got, first_outer), across)
    got = swap(own, by_core)
    grad_w_qkv = jnp.where(first_y, low, high).astype(jnp.float32) + across.astype(jnp.float32)
    return (join(own, got, first_core), grad_w_qkv)


def solution(mesh):
    placed = (P("dp", None), P(), P("dp", "mp"), P(), P(), P("dp", "mp"))
    return jax.shard_map(
        per_device,
        mesh=mesh,
        in_specs=placed,
        out_specs=(P("dp", None), P("dp", "mp")),
        check_vma=False,
    )
```
